128 devices in a mesh: row: 4 (over x), col: 32 (over z, y, core).
Axes of the slice: x: 4, y: 4, z: 4, core: 2. Of those that a mesh axis runs over, the one named last changes fastest.
Arguments:
- sensitivity: bfloat16 [8192, 2, 16384], P('row', None, 'col'), may hold values from -0.25 to 0.25
- sample_weight: float32 [8192], P('row'), may hold values from 0.2 to 5
- pattern: int32 [16, 2, 32], P('row', None, 'col'), may hold values 0 or 1
- prior: float32 [2048], P('row'), may hold values from 0.5 to 5
Outputs:
- factored_band: float32 [2048, 2, 16384], P('row', None, 'col')
The draws below stay inside these ranges and needn't reach their ends.
Inputs may be any that keep to these rules, and one draw needn't show every extreme that they name: pattern holds only 0 and 1.
All inputs are finite; a program needn't handle non-finite values. No bound on the sum of `pattern` on one device may be relied on, other than what follows from the above.
Results may differ from the reference program's by a relative error of at most 0.0028.
Values may be sent and summed in bfloat16 or wider, within the bound.
A program may use at most 128 MiB of HBM per device.

```python
import math
import jax
import jax.numpy as jnp
from jax import lax

TILE = 512
P_SIZE = 32768
SAMPLES = 8192
SBLK = 16
BAND = 2048
CYCLES = 2
N_COL = 32


def set_ends(result, own_key, least, high):
    longest = result.shape.index(max(result.shape))
    spots = []
    for shift in (0, 1):
        where = [jax.random.randint(jax.random.fold_in(own_key, axis), (), 0, length) for axis, length in enumerate(result.shape)]
        where[longest] = (where[longest] + shift) % result.shape[longest]
        spots.append(tuple(where))
    return result.at[spots[0]].set(least).at[spots[1]].set(high)


def steps_of(stream_key, shape, pieces, smallest, largest):
    loudness = 1.0
    for axis_at, parts in pieces:
        draws = jax.random.uniform(jax.random.fold_in(jax.random.fold_in(stream_key, 6), axis_at), (parts,), jnp.float32, smallest / len(pieces), largest / len(pieces))
        loudness = loudness * jnp.repeat(jnp.exp(draws), shape[axis_at] // parts).reshape((-1,) + (1,) * (len(shape) - 1 - axis_at))
    return loudness


def scatter_about(own_key, dims, scale, limit, shards=(), held_as=jnp.bfloat16):
    entries = scale * jax.random.normal(own_key, dims, jnp.float32)
    if shards:
        entries = entries * steps_of(own_key, dims, shards, -0.22, 0.18)
    return jnp.clip(entries, -limit, limit).astype(held_as)


def setup_inputs(seed: int = 0) -> dict:
    arg_keys = jax.random.split(jax.random.key(seed), 5)
    return {
        "sensitivity": scatter_about(arg_keys[0], (SAMPLES, CYCLES, N_COL * TILE), TILE ** -0.5, 0.25, ((0, 4), (2, 32))),
        "sample_weight": jnp.clip(jnp.exp(math.log(5.0) - 3.218876 * jax.random.uniform(arg_keys[1], (SAMPLES,), jnp.float32) ** steps_of(arg_keys[1], (SAMPLES,), ((0, 4),), -0.2, 0.2)), 0.2, 5.0),
        "pattern": set_ends((jax.random.randint(arg_keys[2], (SBLK, CYCLES, N_COL), 0, 2) < 1).astype(jnp.int32), jax.random.fold_in(arg_keys[2], 1), 0, 1),
        "prior": jnp.clip(jnp.exp(math.log(5.0) - 2.3025851 * jax.random.uniform(arg_keys[3], (BAND,), jnp.float32) ** steps_of(arg_keys[3], (BAND,), ((0, 4),), -0.2, 0.2)), 0.5, 5.0),
    }


def reference(sensitivity, sample_weight, pattern, prior):
    blocks = pattern.reshape(SAMPLES // TILE, P_SIZE // TILE).astype(jnp.bfloat16)
    masked = (sensitivity.reshape(SAMPLES // TILE, TILE, P_SIZE // TILE, TILE) * blocks[:, None, :, None]).reshape(SAMPLES, P_SIZE)
    weighted = (sample_weight[:, None] * masked.astype(jnp.float32)).astype(jnp.bfloat16)
    fisher = jnp.dot(masked[:, :BAND].T.astype(jnp.float32), weighted.astype(jnp.float32), preferred_element_type=jnp.float32)
    fisher = fisher.at[:, :BAND].add(jnp.diag(prior))
    lower = jnp.linalg.cholesky(fisher[:TILE, :TILE])
    panel = jax.scipy.linalg.solve_triangular(lower, fisher[:TILE], lower=True)
    updated = fisher[TILE:] - jnp.dot(panel[:, TILE:BAND].T, panel, precision=lax.Precision.HIGHEST)
    return jnp.concatenate([panel, updated], axis=0).reshape(BAND, CYCLES, -1)
```

```python
import jax
import jax.numpy as jnp
from jax import lax
from jax.experimental import pallas as pl
from jax.experimental.pallas import tpu as pltpu
from jax.sharding import PartitionSpec as P

F32 = jnp.float32
BF16 = jnp.bfloat16
HIGHEST = lax.Precision.HIGHEST
MESH = pl.DeviceIdType.MESH
VMEM = pl.BlockSpec(memory_space=pltpu.VMEM)
NCH = 8
CH = 512 // NCH
SKEW = 3
ON = {'band', 'corner', 'mm', 'rs', 'f0', 'f0r', 'ctree'}
TILES = (0, 2, 1, 3)
T = 4 * NCH + 6 * SKEW
NC = 4
NR = 2
SEND = {
    0: {0: ((0, 3, "mid"), (1, 1, "mid")), 3: ((1, 3, "end"),), 1: ((0, 1, "end"),)},
    2: {0: ((0, 3, "mid"), (1, 1, "mid")), 3: ((1, 3, "end"),), 1: ((0, 1, "end"),)},
    1: {3: ((0, 1, "mid"), (1, 1, "mid")), 2: ((0, 3, "end"), (1, 3, "end"))},
    3: {1: ((0, 3, "mid"), (1, 3, "mid")), 2: ((0, 1, "end"), (1, 1, "end"))},
}
MID = {
    0: {3: ((0, 3),), 1: ((1, 1),)},
    2: {3: ((0, 3),), 1: ((1, 1),)},
    1: {0: ((0, 1), (1, 1))},
    3: {0: ((0, 3), (1, 3))},
}
OWNER = {0: 2, 1: 1, 2: 2, 3: 3}


def dotp(a, b, ca=1, cb=0, precision=None):
    return lax.dot_general(
        a, b, (((ca,), (cb,)), ((), ())), precision=precision, preferred_element_type=F32
    )


def loop(n, f, start=0):
    lax.fori_loop(start, n, lambda i, carry: (f(i), carry)[1], 0)


class Place:
    def __init__(self):
        self.row = lax.axis_index("row")
        self.col = lax.axis_index("col")
        self.core = self.col % 2
        self.y = (self.col // 2) % 4
        self.z = self.col // 8
        self.sib = (self.row, self.col + 1 - 2 * self.core)

    def at(self, z, y, core):
        return (self.row, (z * 4 + y) * 2 + core)

    def along(self, step):
        return ((self.row + step) % 4, self.col)


class Tree:
    def __init__(self, pos, q, sy):
        dz, dy = pos.z, (pos.y - sy + 4) % 4
        mz, my = (4 - dz) % 4, (4 - dy) % 4
        u, v = ((dz, dy), (dy, mz), (mz, my), (my, dz))[q]
        fwd = ((0, 1), (3, 0), (0, 3), (1, 0))[q]
        side = ((1, 0), (0, 1), (3, 0), (0, 3))[q]
        back = tuple((4 - d) % 4 for d in fwd)
        other = tuple((4 - d) % 4 for d in side)
        des = q // 2
        to = lambda d: pos.at((pos.z + d[0]) % 4, (pos.y + d[1]) % 4, des)
        self.at_source = (dz == 0) & (dy == 0)
        self.holder = jnp.logical_not(self.at_source) & (pos.core == des)
        depth = jnp.where(u == 0, v, 2 + jnp.where(u == 2, 1, 0) + jnp.where(v == 0, 1, v - 1))
        depth = jnp.where(pos.core == des, depth, depth + 1)
        self.start = SKEW * jnp.where(self.at_source, 1, depth)
        ahead = ((u == 0) & (v < 3)) | ((u >= 1) & ((v == 1) | (v == 2)))
        turn = tuple(jnp.where(u == 0, a, b) for a, b in zip(side, back))
        self.children = (
            (ahead, to(fwd)),
            (v == 1, to(turn)),
            ((v == 1) & ((u == 0) | (u == 3)), to(other)),
        )
        self.root_child = to(fwd)
        self.sib = pos.sib


def copies_of(tree, src, dst, send, recv, idx):
    out = []
    for n, (pred, to) in enumerate(tree.children + ((True, tree.sib),)):
        out.append((pred, pltpu.make_async_remote_copy(
            src, dst, send.at[(n,) + idx], recv.at[idx], device_id=to, device_id_type=MESH
        )))
    return out


def pass_on(tree, copies, do):
    @pl.when(tree.holder)
    def _():
        for pred, copy in copies[:3]:
            pl.when(pred)(getattr(copy, do))
        getattr(copies[3][1], do)()


def set_out(tree, copies, do):
    getattr(copies[0][1], do)()
    getattr(copies[3][1], do)()


def gather_kernel(
    jt, w0, w1, wrow, prior, f_out, f0_out, f0r_out, corner,
    band, pb, rxm, rxd, f0acc, cpart, crx, dg, dgr,
    b_send, b_recv, own_sem, c_send, c_recv, r_send, r_recv,
    rs_sem, rxm_sem, rxd_sem, f0_send, f0_recv, cx_send, cx_recv, dg_send, dg_recv,
):
    pos = Place()
    r, c = pos.row, pos.col

    barrier = pltpu.get_barrier_semaphore()
    greet = [pos.sib, pos.along(1), pos.along(2), pos.along(3)]
    for core in (0, 1):
        for step in (1, 3):
            greet.append(pos.at((pos.z + step) % 4, pos.y, core))
            greet.append(pos.at(pos.z, (pos.y + step) % 4, core))
    for to in greet:
        pl.semaphore_signal(barrier, inc=1, device_id=to, device_id_type=MESH)
    pl.semaphore_wait(barrier, len(greet))

    chips = [[Tree(pos, q, sy) for q in range(4)] for sy in (0, 1)]

    def band_copies(tree, q, i, own=None):
        src = band.at[q, i] if own is None else jt.at[q, pl.ds(pl.multiple_of(own * CH, CH), CH)]
        return copies_of(tree, src, band.at[q, i], b_send, b_recv, (q, i))

    def band_slot(t):
        for n, tile in enumerate(TILES):
            @pl.when((c == tile) & (t >= NCH * n) & (t < NCH * (n + 1)))
            def _():
                for q in range(4):
                    tree = chips[tile // 2][q]
                    set_out(tree, band_copies(tree, q, t, t - NCH * n), "start")
        for sy in (0, 1):
            for q in range(4):
                tree = chips[sy][q]
                i = t - tree.start - NCH * sy

                @pl.when((i >= 0) & (i < 3 * NCH) & ((i < NCH) | (i >= 2 * NCH)))
                def _():
                    @pl.when(c != 2 * sy + jnp.where(i < NCH, 0, 1))
                    def _():
                        copies = band_copies(tree, q, i + NCH * sy)
                        copies[3][1].wait_recv()
                        pass_on(tree, copies, "start")

    def band_sent():
        for n, tile in enumerate(TILES):
            for q in range(4):
                tree = chips[tile // 2][q]

                def done(ch):
                    copies = band_copies(tree, q, NCH * n + ch)
                    pl.when(c == tile)(lambda: set_out(tree, copies, "wait_send"))
                    pass_on(tree, copies, "wait_send")
                loop(NCH, done)

    def own_tile():
        for n, tile in enumerate(TILES):
            @pl.when(c == tile)
            def _():
                for q in range(4):
                    for ch in range(NCH):
                        band[q, NCH * n + ch] = jt[q, CH * ch:CH * (ch + 1)]

    def corner_x(dst, src, i, kind, frm):
        return pltpu.make_async_remote_copy(
            src, dst, cx_send.at[kind, i - 1], cx_recv.at[kind, frm],
            device_id=pos.along(i), device_id_type=MESH,
        )

    def corner_part():
        @pl.when(c == 0)
        def _():
            a = lax.broadcasted_iota(jnp.int32, (128, 512), 0)
            b = lax.broadcasted_iota(jnp.int32, (128, 512), 1)
            for i in range(4):
                acc = jnp.where((b == a + 128 * i) & (r == 0), prior[...], 0.0)
                for q in range(4):
                    acc += dotp(jt[q, 128 * i:128 * (i + 1), :], w0[q])
                cpart[i] = acc
            for i in (1, 2, 3):
                corner_x(crx.at[r], cpart.at[(r + i) % 4], i, 0, r).start()

    def corner_sum():
        @pl.when(c == 0)
        def _():
            total = cpart[r]
            for i in (1, 2, 3):
                frm = (r + i) % 4
                corner_x(crx.at[frm], crx.at[frm], i, 0, frm).wait_recv()
                total += crx[frm]
            corner[r] = total
            for i in (1, 2, 3):
                corner_x(corner.at[r], corner.at[r], i, 1, r).start()

    def corner_take():
        @pl.when(c == 0)
        def _():
            for i in (1, 2, 3):
                frm = (r + i) % 4
                corner_x(corner.at[frm], corner.at[frm], i, 1, frm).wait_recv()

    def corner_sent():
        @pl.when(c == 0)
        def _():
            for i in (1, 2, 3):
                corner_x(crx.at[r], cpart.at[(r + i) % 4], i, 0, r).wait_send()
                corner_x(corner.at[r], corner.at[r], i, 1, r).wait_send()

    def corner_copies(q, ch):
        n = 128 // NC
        ref = corner.at[q, pl.ds(pl.multiple_of(ch * n, n), n)]
        return copies_of(chips[0][q], ref, ref, c_send, c_recv, (q, ch))

    def corner_slot(t):
        @pl.when((c == 0) & (t < NC))
        def _():
            for q in range(4):
                set_out(chips[0][q], corner_copies(q, t), "start")
        for q in range(4):
            i = t - chips[0][q].start

            @pl.when((c != 0) & (i >= 0) & (i < NC))
            def _():
                copies = corner_copies(q, i)
                copies[3][1].wait_recv()
                pass_on(chips[0][q], copies, "start")

    rtrees = [Tree(pos, q, r // 2) for q in range(4)]

    def f0r_copies(q, ch, own=False):
        n = 128 // NR
        rows = pl.ds(pl.multiple_of(q * 128 + ch * n, n), n)
        src = f0_out.at[0, rows] if own else f0r_out.at[rows]
        return copies_of(rtrees[q], src, f0r_out.at[rows], r_send, r_recv, (q, ch))

    def f0r_slot(t):
        @pl.when((c == r) & (t < NR))
        def _():
            for q in range(4):
                set_out(rtrees[q], f0r_copies(q, t, True), "start")
        for q in range(4):
            i = t - rtrees[q].start

            @pl.when((c != r) & (i >= 0) & (i < NR))
            def _():
                copies = f0r_copies(q, i)
                copies[3][1].wait_recv()
                pass_on(rtrees[q], copies, "start")

    def f0r_own():
        @pl.when(c == r)
        def _():
            f0r_out[...] = f0_out[0]

    def trees_sent():
        for q in range(4):
            for n, at, tree, copies in (
                (NC, 0, chips[0][q], corner_copies), (NR, r, rtrees[q], f0r_copies),
            ):
                if ('ctree' if n == NC else 'f0r') not in ON:
                    continue
                for ch in range(n):
                    cp = copies(q, ch)
                    pl.when(c == at)(lambda: set_out(tree, cp, "wait_send"))
                    pl.when(c != at)(lambda: pass_on(tree, cp, "wait_send"))

    def tile_of(k, q):
        n = TILES.index(k)
        return band[q, NCH * n:NCH * (n + 1)].reshape(512, 512)

    def piece(k, half, n):
        cols = pl.ds(pl.multiple_of(n * 256, 256), 256)
        w = (w0, w1)[half]
        acc = dotp(tile_of(k, 0), w[0, :, cols])
        for q in range(1, 4):
            acc += dotp(tile_of(k, q), w[q, :, cols])
        own = r == OWNER[k]

        def put(value):
            @pl.when(own)
            def _():
                if k == 0:
                    f0acc[half, :, cols] = value
                else:
                    f_out[half, :, cols] = value

            @pl.when(jnp.logical_not(own))
            def _():
                pb[k, half, :, cols] = value.astype(BF16)

        if k == 0 or half == 1:
            put(acc)
            return

        @pl.when(c == 0)
        def _():
            value = acc
            first = pl.ds(pl.multiple_of(n * (NCH // 2), NCH // 2), NCH // 2)
            for q in range(4):
                wk = (tile_of(k, q).astype(F32) * wrow[q]).astype(BF16)
                value = value - dotp(wk, band[q, first].reshape(256, 512), 1, 1)
            put(value)

        @pl.when(c == k)
        def _():
            a = lax.broadcasted_iota(jnp.int32, (512, 256), 0)
            b = lax.broadcasted_iota(jnp.int32, (512, 256), 1)
            on = a == b + n * 256
            line = jnp.sum(jnp.where(on, acc, 0.0), axis=0, keepdims=True)
            dg[:, cols] = jnp.broadcast_to(line, (8, 256))
            put(jnp.where(on, 0.0, acc))

        pl.when((c != 0) & (c != k))(lambda: put(acc))

    def dg_copy(i, frm):
        return pltpu.make_async_remote_copy(
            dg, dgr.at[frm], dg_send, dg_recv.at[frm], device_id=pos.along(i), device_id_type=MESH
        )

    def move(k, half, step, kind):
        e = 0 if k == 0 else 1
        side = 0 if step == 3 else 1
        dst, sem = (
            (rxm.at[k, half], rxm_sem.at[k, half]) if kind == "mid"
            else (rxd.at[e, side, half], rxd_sem.at[e, side, half])
        )
        return pltpu.make_async_remote_copy(
            pb.at[k, half], dst, rs_sem.at[k, half], sem, device_id=pos.along(step), device_id_type=MESH
        )

    def rs_send(k):
        for row, moves in SEND[k].items():
            @pl.when(r == row)
            def _():
                for m in moves:
                    move(k, *m).start()
        if k:
            for i in (1, 2, 3):
                pl.when((c == k) & ((r + i) % 4 == k))(dg_copy(i, r).start)

    def rs_mid(k):
        for row, moves in MID[k].items():
            @pl.when(r == row)
            def _():
                for half, step in moves:
                    move(k, half, step, "mid").wait_recv()
                    pb[k, half] = (pb[k, half].astype(F32) + rxm[k, half].astype(F32)).astype(BF16)
                    move(k, half, step, "end").start()

    def rs_end(k):
        e = 0 if k == 0 else 1

        @pl.when(r == OWNER[k])
        def _():
            for half in (0, 1):
                for step in (1, 3):
                    move(k, half, step, "end").wait_recv()
                got = rxd[e, 0, half].astype(F32) + rxd[e, 1, half].astype(F32)
                if k == 0:
                    f0_out[half] = (f0acc[half] + got).astype(BF16)
                    for step in (1, 3):
                        if 'f0' in ON: f0_copy(half, step).start()
                else:
                    f_out[half] = f_out[half] + got
            if k == 0:
                return

            @pl.when(c == k)
            def _():
                line = prior[...]
                for i in (1, 2, 3):
                    frm = (r + i) % 4
                    dg_copy(i, frm).wait_recv()
                    line = line + dgr[frm, 0:1, :]
                a = lax.broadcasted_iota(jnp.int32, (512, 512), 0)
                b = lax.broadcasted_iota(jnp.int32, (512, 512), 1)
                own = jnp.sum(jnp.where(a == b, f_out[0], 0.0), axis=0, keepdims=True)
                own = own + dg[0:1, :]
                f_out[0] = jnp.where(a == b, own + line, f_out[0])

    def rs_sent(k):
        for table in (SEND, MID):
            for row, moves in table[k].items():
                @pl.when(r == row)
                def _():
                    for m in moves:
                        move(k, m[0], m[1], "end").wait_send()
        if k:
            for i in (1, 2, 3):
                pl.when((c == k) & ((r + i) % 4 == k))(dg_copy(i, r).wait_send)

    def f0_copy(half, step):
        return pltpu.make_async_remote_copy(
            f0_out.at[half], f0_out.at[half], f0_send.at[half, step // 2], f0_recv.at[half],
            device_id=pos.along(step), device_id_type=MESH,
        )

    def f0_pass():
        @pl.when(r != 2)
        def _():
            for half in (0, 1):
                f0_copy(half, 1).wait_recv()
        pl.when(r == 1)(f0_copy(0, 3).start)
        pl.when(r == 3)(f0_copy(1, 1).start)

    def f0_sent():
        @pl.when(r == 2)
        def _():
            for half in (0, 1):
                for step in (1, 3):
                    f0_copy(half, step).wait_send()
        pl.when(r == 1)(f0_copy(0, 3).wait_send)
        pl.when(r == 3)(f0_copy(1, 1).wait_send)

    RS, MM, BA, CO, CT = ('rs' in ON), ('mm' in ON), ('band' in ON), ('corner' in ON), ('ctree' in ON)
    C0 = 22

    def slots(a, b):
        def one(t):
            if BA:
                band_slot(t)
            if CT:
                pl.when((t >= C0) & (t < C0 + NC + 6 * SKEW))(lambda: corner_slot(t - C0))
        loop(b, one, a)

    def product(k, t=None):
        for half in (0, 1):
            def one(n):
                if MM: piece(k, half, n)
                if t is not None and BA:
                    band_slot(t + 2 * half + n)
                if t is not None and CT:
                    corner_slot(t + 2 * half + n - C0)
            loop(2, one)

    slots(0, 2)
    if CO: corner_part()
    slots(2, 12)
    if BA: own_tile()
    if CO: corner_sum()
    slots(12, C0)
    if CO: corner_take()
    slots(C0, 26)
    product(0, 26)
    if RS: rs_send(0)
    slots(30, 34)
    product(2, 34)
    if RS: rs_send(2)
    if RS: rs_mid(0)
    slots(38, 42)
    product(1, 42)
    if RS:
        rs_send(1)
        rs_mid(2)
        rs_end(0)
    slots(46, T)
    product(3)
    if RS:
        rs_send(3)
        rs_mid(1)
        rs_mid(3)
    if 'f0' in ON: f0_pass()
    if 'f0r' in ON:
        loop(NR + 6 * SKEW, f0r_slot)
        f0r_own()
    if RS:
        for k in (1, 2, 3):
            rs_end(k)

    if BA: band_sent()
    trees_sent()
    if RS:
        for k in range(4):
            rs_sent(k)
    if 'f0' in ON: f0_sent()
    if CO: corner_sent()


def gather(jt, w0, w1, wrow, prior):
    dma = pltpu.SemaphoreType.DMA
    return pl.pallas_call(
        gather_kernel,
        out_shape=[
            jax.ShapeDtypeStruct((2, 512, 512), F32),
            jax.ShapeDtypeStruct((2, 512, 512), BF16),
            jax.ShapeDtypeStruct((512, 512), BF16),
            jax.ShapeDtypeStruct((4, 128, 512), F32),
        ],
        in_specs=[VMEM] * 5,
        out_specs=[VMEM] * 4,
        scratch_shapes=[
            pltpu.VMEM((4, 4 * NCH, CH, 512), BF16),
            pltpu.VMEM((4, 2, 512, 512), BF16),
            pltpu.VMEM((4, 2, 512, 512), BF16),
            pltpu.VMEM((2, 2, 2, 512, 512), BF16),
            pltpu.VMEM((2, 512, 512), F32),
            pltpu.VMEM((4, 128, 512), F32),
            pltpu.VMEM((4, 128, 512), F32),
            pltpu.VMEM((8, 512), F32),
            pltpu.VMEM((4, 8, 512), F32),
            dma((4, 4, 4 * NCH)), dma((4, 4 * NCH)), dma,
            dma((4, 4, NC)), dma((4, NC)), dma((4, 4, NR)), dma((4, NR)),
            dma((4, 2)), dma((4, 2)), dma((2, 2, 2)), dma((2, 2)), dma((2,)),
            dma((2, 3)), dma((2, 4)), dma, dma((4,)),
        ],
        compiler_params=pltpu.CompilerParams(
            collective_id=0, has_side_effects=True, vmem_limit_bytes=58 * 2**20
        ),
        cost_estimate=pl.CostEstimate(flops=2 * 2048 * 2048 * 1024, bytes_accessed=2**24, transcendentals=0),
    )(jt, w0, w1, wrow, prior)


def split3(x):
    a = x.astype(BF16)
    rest = x - a.astype(F32)
    b = rest.astype(BF16)
    return a, b, (rest - b.astype(F32)).astype(BF16)


def invert_tile(m, size=16):
    lane = lax.broadcasted_iota(jnp.int32, (size, 128), 1)
    row = lax.broadcasted_iota(jnp.int32, (size, 128), 0)
    rows = lax.broadcasted_iota(jnp.int32, (128, 128), 0)
    lanes = lax.broadcasted_iota(jnp.int32, (128, 128), 1)
    spread = lambda v: jnp.broadcast_to(v, (size, 128))

    def panel(p, m):
        active = 128 - size * p
        x = m[:size]
        cols = [spread(x[:, j:j + 1]) for j in range(size)]
        pivots = jnp.zeros((size, 128), F32)
        d = spread(cols[0][0:1])
        for j in range(size):
            q = pl.reciprocal(d, approx=True)
            q = q * (2.0 - d * q)
            pivots = jnp.where(row == j, d, pivots)
            below = jnp.where(row > j, cols[j], 0.0)
            if j + 1 < size:
                d = spread(cols[j + 1][j + 1:j + 2]) - q * (
                    spread(cols[j][j + 1:j + 2]) * spread(cols[j + 1][j:j + 1])
                )
            u = spread(jnp.where(lane[:1] == j, 1.0, x[j:j + 1]))
            x = jnp.where((lane == j) & (row >= j), jnp.where(row == j, 1.0, 0.0), x)
            x = x - q * (below * u)
            for k in range(j + 1, size):
                cols[k] = cols[k] - q * (below * spread(cols[k][j:j + 1]))
        s = lax.rsqrt(pivots)
        x = x * (s * (1.5 - 0.5 * pivots * s * s))
        x = jnp.where((lane < size) & (lane > row), 0.0, x)
        left = jnp.where((lane >= size) & (lane < active), x, 0.0)
        x1, x2, x3 = split3(x)
        y1, y2, y3 = split3(left)
        update = dotp(
            jnp.concatenate([y1, y1, y2, y2, y1, y3], axis=0),
            jnp.concatenate([x1, x2, x1, x2, x3, x1], axis=0), 0, 0,
        )
        m = jnp.where((lanes < size) & (rows < active), 0.0, m) - update
        m = jnp.concatenate([m[size:], x], axis=0)
        return pltpu.roll(m, 128 - size, 1)

    m = lax.fori_loop(0, 128 // size, panel, m)
    return jnp.where(rows >= lanes, m, 0.0)


def invert_factor(a):
    for j in range(4):
        here = slice(128 * j, 128 * (j + 1))
        t = invert_tile(a[here, here])
        a[here, here] = t
        if j > 0:
            a[here, 0:128 * j] = dotp(t, a[here, 0:128 * j], precision=HIGHEST)
        if j < 3:
            low = 128 * (j + 1)
            a[here, low:] = dotp(t, a[here, low:], precision=HIGHEST)
            u = a[here, :]
            lanes = lax.broadcasted_iota(jnp.int32, (512 - low, 512), 1)
            kept = jnp.where((lanes >= 128 * j) & (lanes < low), 0.0, a[low:, :])
            a[low:, :] = kept - dotp(u[:, low:], u, 0, 0, precision=HIGHEST)
    a_rows = lax.broadcasted_iota(jnp.int32, (512, 512), 0)
    a_lanes = lax.broadcasted_iota(jnp.int32, (512, 512), 1)
    a[...] = jnp.where(a_rows >= a_lanes, a[...], 0.0)


def dot3(a, b, ca=1, cb=0):
    return dotp(a[0], b[0], ca, cb) + (dotp(a[0], b[1], ca, cb) + dotp(a[1], b[0], ca, cb))


def pair(x):
    a = x.astype(BF16)
    return a, (x - a.astype(F32)).astype(BF16)


def factor_kernel(f, f0, f0r, corner, out, a, res, sem):
    r, c = lax.axis_index("row"), lax.axis_index("col")
    for q in range(4):
        a[128 * q:128 * (q + 1), :] = corner[q]
    invert_factor(a)
    linv = pair(a[...])

    def put(half):
        return pltpu.make_async_copy(res.at[half], out.at[:, half, :], sem.at[half])

    def panel(half):
        return dotp(linv[0], f0[half]) + dotp(linv[1], f0[half])

    @pl.when(r == 0)
    def _():
        @pl.when(c == 0)
        def _():
            res[0] = dot3(linv, pair(corner[...].reshape(512, 512)))

        @pl.when(c != 0)
        def _():
            res[0] = panel(0)
        put(0).start()
        res[1] = panel(1)
        put(1).start()

    @pl.when(r != 0)
    def _():
        right = pair(dotp(linv[0], f0r[...]) + dotp(linv[1], f0r[...]))

        @pl.when(c == 0)
        def _():
            res[0] = f[0]

        @pl.when(c != 0)
        def _():
            res[0] = f[0] - dot3(right, pair(panel(0)), 0, 0)
        put(0).start()
        res[1] = f[1] - dot3(right, pair(panel(1)), 0, 0)
        put(1).start()

    for half in (0, 1):
        put(half).wait()


def factor(f, f0, f0r, corner):
    return pl.pallas_call(
        factor_kernel,
        out_shape=jax.ShapeDtypeStruct((512, 2, 512), F32),
        in_specs=[VMEM] * 4,
        out_specs=pl.BlockSpec(memory_space=pl.ANY),
        scratch_shapes=[
            pltpu.VMEM((512, 512), F32),
            pltpu.VMEM((2, 512, 512), F32),
            pltpu.SemaphoreType.DMA((2,)),
        ],
        compiler_params=pltpu.CompilerParams(vmem_limit_bytes=56 * 2**20),
        cost_estimate=pl.CostEstimate(flops=2**31, bytes_accessed=2**23, transcendentals=0),
    )(f, f0, f0r, corner)


def body(sensitivity, sample_weight, pattern, prior):
    blocks = pattern.shape[0]
    x = sensitivity.reshape(blocks * 512, 1024)
    mask = jnp.repeat(pattern[:, :, 0].astype(F32), 512, axis=0)
    scale = sample_weight[:, None] * mask
    w = [
        (scale[:, i:i + 1] * x[:, 512 * i:512 * (i + 1)].astype(F32)).astype(BF16).reshape(blocks, 512, 512)
        for i in (0, 1)
    ]
    jt = (x[:, :512] * mask[:, 0:1].astype(BF16)).reshape(blocks, 512, 512).transpose(0, 2, 1)
    f, f0, f0r, corner = gather(
        jt, w[0], w[1], sample_weight.reshape(blocks, 1, 512), prior.reshape(1, 512)
    )
    return factor(f, f0, f0r, corner)


def solution(mesh):
    return jax.shard_map(
        body,
        mesh=mesh,
        in_specs=(P("row", None, "col"), P("row"), P("row", None, "col"), P("row")),
        out_specs=P("row", None, "col"),
        check_vma=False,
    )
```

```python
import jax
import jax.numpy as jnp
from jax import lax
from jax.experimental import pallas as pl
from jax.experimental.pallas import tpu as pltpu
from jax.sharding import PartitionSpec as P

F32 = jnp.float32
BF16 = jnp.bfloat16
HIGHEST = lax.Precision.HIGHEST
MESH = pl.DeviceIdType.MESH
VMEM = pl.BlockSpec(memory_space=pltpu.VMEM)
NCH = 8
CH = 512 // NCH
SKEW = 4
TILES = (0, 2, 1, 3)
T = 4 * NCH + 5 * SKEW
SKEWR = 4
NC = 4
NR = 2
SEND = {
    0: {0: ((0, 3, "mid"), (1, 1, "mid")), 3: ((1, 3, "end"),), 1: ((0, 1, "end"),)},
    2: {0: ((0, 3, "mid"), (1, 1, "mid")), 3: ((1, 3, "end"),), 1: ((0, 1, "end"),)},
    1: {3: ((0, 1, "mid"), (1, 1, "mid")), 2: ((0, 3, "end"), (1, 3, "end"))},
    3: {1: ((0, 3, "mid"), (1, 3, "mid")), 2: ((0, 1, "end"), (1, 1, "end"))},
}
MID = {
    0: {3: ((0, 3),), 1: ((1, 1),)},
    2: {3: ((0, 3),), 1: ((1, 1),)},
    1: {0: ((0, 1), (1, 1))},
    3: {0: ((0, 3), (1, 3))},
}
OWNER = {0: 2, 1: 1, 2: 2, 3: 3}


def dotp(a, b, ca=1, cb=0, precision=None):
    return lax.dot_general(
        a, b, (((ca,), (cb,)), ((), ())), precision=precision, preferred_element_type=F32
    )


def loop(n, f, start=0):
    lax.fori_loop(start, n, lambda i, carry: (f(i), carry)[1], 0)


class Place:
    def __init__(self):
        self.row = lax.axis_index("row")
        self.col = lax.axis_index("col")
        self.core = self.col % 2
        self.y = (self.col // 2) % 4
        self.z = self.col // 8
        self.sib = (self.row, self.col + 1 - 2 * self.core)

    def at(self, z, y, core):
        return (self.row, (z * 4 + y) * 2 + core)

    def along(self, step):
        return ((self.row + step) % 4, self.col)


class Tree:
    def __init__(self, pos, m, sy, skew):
        dz, dy = pos.z, (pos.y - sy + 4) % 4
        mz, my = (4 - dz) % 4, (4 - dy) % 4
        first = pos.core == 0
        pick = lambda table: tuple(
            jnp.where(first, a, b) for a, b in zip(table[m], table[2 + m])
        )
        u, v = pick(((dz, dy), (dy, mz), (mz, my), (my, dz)))
        fwd = pick(((0, 1), (3, 0), (0, 3), (1, 0)))
        side = pick(((1, 0), (0, 1), (3, 0), (0, 3)))
        back = tuple((4 - d) % 4 for d in fwd)
        other = tuple((4 - d) % 4 for d in side)
        to = lambda d: pos.at((pos.z + d[0]) % 4, (pos.y + d[1]) % 4, pos.core)
        self.q = 2 * pos.core + m
        self.at_source = (dz == 0) & (dy == 0)
        depth = jnp.where(u == 0, v, 2 + jnp.where(u == 2, 1, 0) + jnp.where(v == 0, 1, v - 1))
        self.start = jnp.where(self.at_source, -1000, skew * depth)
        ahead = ((u == 0) & (v < 3)) | ((u >= 1) & ((v == 1) | (v == 2)))
        turn = tuple(jnp.where(u == 0, a, b) for a, b in zip(side, back))
        self.children = (
            (ahead, to(fwd)),
            (v == 1, to(turn)),
            ((v == 1) & ((u == 0) | (u == 3)), to(other)),
        )


class Spread:
    def __init__(self, pos, sy, column, n, src, dst, send, recv, sib_send, sib_recv, skew=SKEW):
        self.pos, self.column, self.n = pos, column, n
        self.trees = [Tree(pos, m, sy, skew) for m in (0, 1)]
        self.dst, self.send, self.recv = dst, send, recv
        self.sib_send, self.sib_recv = sib_send, sib_recv
        self.src = src
        self.mine = pos.col == column
        self.sy = sy

    def children(self, tree, i):
        q = tree.q
        return [
            (pred, pltpu.make_async_remote_copy(
                self.dst(q, i, 1), self.dst(q, i, 1), self.send.at[k, q, i], self.recv.at[q, i],
                device_id=to, device_id_type=MESH))
            for k, (pred, to) in enumerate(tree.children)
        ]

    def root(self, q, i):
        step = ((0, 1), (3, 0), (0, 3), (1, 0))[q]
        pos = self.pos
        return pltpu.make_async_remote_copy(
            self.src(q, i, 1), self.dst(q, i, 1), self.send.at[0, q, i], self.recv.at[q, i],
            device_id=pos.at(step[0], (self.sy + step[1]) % 4, q // 2), device_id_type=MESH)

    def sibling(self, q, src):
        return pltpu.make_async_remote_copy(
            src(q, 0, self.n), self.dst(q, 0, self.n), self.sib_send.at[q], self.sib_recv.at[q],
            device_id=self.pos.sib, device_id_type=MESH)

    def begin(self, t):
        @pl.when(self.mine & (t >= 0) & (t < self.n))
        def _():
            for q in range(4):
                self.root(q, t).start()

            @pl.when(t == self.n - 1)
            def _():
                for q in range(4):
                    self.sibling(q, self.src).start()

    def slot(self, t):
        self.begin(t)
        for tree in self.trees:
            i = t - tree.start

            @pl.when((i >= 0) & (i < self.n))
            def _():
                copies = self.children(tree, i)
                copies[0][1].wait_recv()
                for pred, copy in copies:
                    pl.when(pred)(copy.start)
                pl.when(i == self.n - 1)(lambda: self.sibling(tree.q, self.dst).start())

    def take(self):
        away = jnp.logical_not(self.trees[0].at_source)
        other = 1 - self.pos.core
        for q in range(4):
            @pl.when((away & (other == q // 2)) | (self.trees[0].at_source & jnp.logical_not(self.mine)))
            def _():
                self.sibling(q, self.dst).wait_recv()

    def sent(self):
        @pl.when(self.mine)
        def _():
            for q in range(4):
                loop(self.n, lambda i: self.root(q, i).wait_send())
                self.sibling(q, self.src).wait_send()
        for tree in self.trees:
            @pl.when(jnp.logical_not(tree.at_source))
            def _():
                def one(i):
                    for pred, copy in self.children(tree, i):
                        pl.when(pred)(copy.wait_send)
                loop(self.n, one)
                self.sibling(tree.q, self.dst).wait_send()


def gather_kernel(
    jt, w0, w1, wrow, prior, f_out, f0_out, f0r_out, corner, linv,
    band, pb, rxm, rxd, f0acc, cpart, crx, dg, dgr,
    b_send, b_recv, bs_send, bs_recv, c_send, c_recv, cs_send, cs_recv,
    r_send, r_recv, rs_send2, rs_recv2,
    rs_sem, rxm_sem, rxd_sem, f0_send, f0_recv, cx_send, cx_recv, dg_send, dg_recv,
):
    pos = Place()
    r, c = pos.row, pos.col

    barrier = pltpu.get_barrier_semaphore()
    greet = [pos.sib, pos.along(1), pos.along(2), pos.along(3)]
    for core in (0, 1):
        for step in (1, 3):
            greet.append(pos.at((pos.z + step) % 4, pos.y, core))
            greet.append(pos.at(pos.z, (pos.y + step) % 4, core))
    for to in greet:
        pl.semaphore_signal(barrier, inc=1, device_id=to, device_id_type=MESH)
    pl.semaphore_wait(barrier, len(greet))

    def run(q, i, n, rows):
        return pl.ds(pl.multiple_of((q * 0 + i) * rows, rows), n * rows)

    bands = []
    for n, tile in enumerate(TILES):
        bands.append(Spread(
            pos, tile // 2, tile, NCH,
            lambda q, i, m: jt.at[q, run(q, i, m, CH)],
            lambda q, i, m, n=n: band.at[q, n, run(q, i, m, CH)],
            b_send.at[n], b_recv.at[n], bs_send.at[n], bs_recv.at[n]))

    def corner_rows(q, i, m):
        return corner.at[q, run(q, i, m, 128 // NC)]

    corners = Spread(pos, 0, 0, NC, corner_rows, corner_rows, c_send, c_recv, cs_send, cs_recv)

    def f0r_rows(ref):
        return lambda q, i, m: ref.at[pl.ds(
            pl.multiple_of(q * 128 + i * (128 // NR), 128 // NR), m * (128 // NR))]

    f0rs = Spread(pos, r // 2, r, NR, f0r_rows(f0_out.at[0]), f0r_rows(f0r_out),
                  r_send, r_recv, rs_send2, rs_recv2, SKEWR)

    def band_slot(t):
        for n in range(4):
            @pl.when((t >= NCH * n) & (t < NCH * (n + 1) + 5 * SKEW))
            def _():
                bands[n].slot(t - NCH * n)

    def corner_slot(t):
        corners.slot(t)

    def f0r_slot(t):
        f0rs.slot(t)

    def own_tile():
        for n, tile in enumerate(TILES):
            @pl.when(c == tile)
            def _():
                for q in range(4):
                    band[q, n] = jt[q]

    def corner_x(dst, src, i, kind, frm):
        return pltpu.make_async_remote_copy(
            src, dst, cx_send.at[kind, i - 1], cx_recv.at[kind, frm],
            device_id=pos.along(i), device_id_type=MESH,
        )

    def corner_part():
        @pl.when(c == 0)
        def _():
            a = lax.broadcasted_iota(jnp.int32, (128, 512), 0)
            b = lax.broadcasted_iota(jnp.int32, (128, 512), 1)
            for i in range(4):
                acc = jnp.where((b == a + 128 * i) & (r == 0), prior[...], 0.0)
                for q in range(4):
                    acc += dotp(jt[q, 128 * i:128 * (i + 1), :], w0[q])
                cpart[i] = acc
            for i in (1, 2, 3):
                corner_x(crx.at[r], cpart.at[(r + i) % 4], i, 0, r).start()

    def corner_sum():
        @pl.when(c == 0)
        def _():
            total = cpart[r]
            for i in (1, 2, 3):
                frm = (r + i) % 4
                corner_x(crx.at[frm], crx.at[frm], i, 0, frm).wait_recv()
                total += crx[frm]
            corner[r] = total
            for i in (1, 2, 3):
                corner_x(corner.at[r], corner.at[r], i, 1, r).start()

    def corner_take():
        @pl.when(c == 0)
        def _():
            for i in (1, 2, 3):
                frm = (r + i) % 4
                corner_x(corner.at[frm], corner.at[frm], i, 1, frm).wait_recv()

    def corner_sent():
        @pl.when(c == 0)
        def _():
            for i in (1, 2, 3):
                corner_x(crx.at[r], cpart.at[(r + i) % 4], i, 0, r).wait_send()
                corner_x(corner.at[r], corner.at[r], i, 1, r).wait_send()

    def f0r_own():
        @pl.when(c == r)
        def _():
            f0r_out[...] = f0_out[0]

    def tile_of(k, q):
        return band[q, TILES.index(k)]

    def piece(k, half, n):
        cols = pl.ds(pl.multiple_of(n * 256, 256), 256)
        w = (w0, w1)[half]
        acc = dotp(tile_of(k, 0), w[0, :, cols])
        for q in range(1, 4):
            acc += dotp(tile_of(k, q), w[q, :, cols])
        own = r == OWNER[k]

        def put(value):
            @pl.when(own)
            def _():
                if k == 0:
                    f0acc[half, :, cols] = value
                else:
                    f_out[half, :, cols] = value

            @pl.when(jnp.logical_not(own))
            def _():
                pb[k, half, :, cols] = value.astype(BF16)

        if k == 0 or half == 1:
            put(acc)
            return

        @pl.when(c == 0)
        def _():
            value = acc
            first = pl.ds(pl.multiple_of(n * 256, 256), 256)
            for q in range(4):
                wk = (tile_of(k, q).astype(F32) * wrow[q]).astype(BF16)
                value = value - dotp(wk, band[q, 0, first], 1, 1)
            put(value)

        @pl.when(c == k)
        def _():
            a = lax.broadcasted_iota(jnp.int32, (512, 256), 0)
            b = lax.broadcasted_iota(jnp.int32, (512, 256), 1)
            on = a == b + n * 256
            line = jnp.sum(jnp.where(on, acc, 0.0), axis=0, keepdims=True)
            dg[:, cols] = jnp.broadcast_to(line, (8, 256))
            put(jnp.where(on, 0.0, acc))

        pl.when((c != 0) & (c != k))(lambda: put(acc))

    def dg_copy(i, frm):
        return pltpu.make_async_remote_copy(
            dg, dgr.at[frm], dg_send, dg_recv.at[frm], device_id=pos.along(i), device_id_type=MESH
        )

    def move(k, half, step, kind):
        e = 0 if k == 0 else 1
        side = 0 if step == 3 else 1
        dst, sem = (
            (rxm.at[k, half], rxm_sem.at[k, half]) if kind == "mid"
            else (rxd.at[e, side, half], rxd_sem.at[e, side, half])
        )
        return pltpu.make_async_remote_copy(
            pb.at[k, half], dst, rs_sem.at[k, half], sem, device_id=pos.along(step), device_id_type=MESH
        )

    def rs_send(k):
        for row, moves in SEND[k].items():
            @pl.when(r == row)
            def _():
                for m in moves:
                    move(k, *m).start()
        if k:
            for i in (1, 2, 3):
                pl.when((c == k) & ((r + i) % 4 == k))(dg_copy(i, r).start)

    def rs_mid(k):
        for row, moves in MID[k].items():
            @pl.when(r == row)
            def _():
                for half, step in moves:
                    move(k, half, step, "mid").wait_recv()
                    pb[k, half] = (pb[k, half].astype(F32) + rxm[k, half].astype(F32)).astype(BF16)
                    move(k, half, step, "end").start()

    def rs_end(k):
        e = 0 if k == 0 else 1

        @pl.when(r == OWNER[k])
        def _():
            for half in (0, 1):
                for step in (1, 3):
                    move(k, half, step, "end").wait_recv()
                got = rxd[e, 0, half].astype(F32) + rxd[e, 1, half].astype(F32)
                if k == 0:
                    f0_out[half] = (f0acc[half] + got).astype(BF16)
                    for step in (1, 3):
                        f0_copy(half, step).start()
                else:
                    f_out[half] = f_out[half] + got
            if k == 0:
                return

            @pl.when(c == k)
            def _():
                line = prior[...]
                for i in (1, 2, 3):
                    frm = (r + i) % 4
                    dg_copy(i, frm).wait_recv()
                    line = line + dgr[frm, 0:1, :]
                a = lax.broadcasted_iota(jnp.int32, (512, 512), 0)
                b = lax.broadcasted_iota(jnp.int32, (512, 512), 1)
                own = jnp.sum(jnp.where(a == b, f_out[0], 0.0), axis=0, keepdims=True)
                own = own + dg[0:1, :]
                f_out[0] = jnp.where(a == b, own + line, f_out[0])

    def rs_sent(k):
        for table in (SEND, MID):
            for row, moves in table[k].items():
                @pl.when(r == row)
                def _():
                    for m in moves:
                        move(k, m[0], m[1], "end").wait_send()
        if k:
            for i in (1, 2, 3):
                pl.when((c == k) & ((r + i) % 4 == k))(dg_copy(i, r).wait_send)

    def f0_copy(half, step):
        return pltpu.make_async_remote_copy(
            f0_out.at[half], f0_out.at[half], f0_send.at[half, step // 2], f0_recv.at[half],
            device_id=pos.along(step), device_id_type=MESH,
        )

    def f0_take(half, rows):
        for row in rows:
            pl.when(r == row)(f0_copy(half, 1).wait_recv)
        if half == 0:
            if 1 in rows: pl.when(r == 1)(f0_copy(0, 3).start)
        elif 3 in rows:
            pl.when(r == 3)(f0_copy(1, 1).start)

    def f0_sent():
        @pl.when(r == 2)
        def _():
            for half in (0, 1):
                for step in (1, 3):
                    f0_copy(half, step).wait_send()
        pl.when(r == 1)(f0_copy(0, 3).wait_send)
        pl.when(r == 3)(f0_copy(1, 1).wait_send)

    C0 = 20

    def both(t):
        band_slot(t)
        pl.when((t >= C0) & (t < C0 + NC + 5 * SKEW))(lambda: corner_slot(t - C0))

    def slots(a, b):
        loop(b, both, a)

    def product(k, t=None):
        bands[TILES.index(k)].take()
        for half in (0, 1):
            def one(n):
                piece(k, half, n)
                if t is not None: both(t + 2 * half + n)
            loop(2, one)

    slots(0, 2)
    corner_part()
    slots(2, 12)
    own_tile()
    corner_sum()
    slots(12, C0)
    corner_take()
    P0 = NCH + 5 * SKEW
    slots(C0, P0 + 1)
    product(0, P0 + 1)
    rs_send(0)
    slots(P0 + 5, P0 + NCH + 1)
    product(2, P0 + NCH + 1)
    rs_send(2)
    rs_mid(0)
    slots(P0 + NCH + 5, P0 + 2 * NCH + 1)
    product(1, P0 + 2 * NCH + 1)
    rs_send(1)
    rs_mid(2)
    rs_end(0)
    slots(P0 + 2 * NCH + 5, T)
    product(3)
    corners.take()
    rs_send(3)
    rs_mid(1)
    for q in range(4):
        linv[128 * q:128 * (q + 1), :] = corner[q]
    beside = lambda j: lambda p: pl.when(r != 0)(lambda: f0r_slot(p + 8 * j))
    invert_step(linv, 0)
    rs_mid(3)
    invert_step(linv, 1)
    f0_take(0, (1, 3))
    invert_step(linv, 2, beside(0))
    f0_take(1, (1, 3))
    invert_step(linv, 3, beside(1))

    @pl.when(r != 0)
    def _():
        loop(NR + 5 * SKEWR, f0r_slot, 16)
        f0r_own()
        f0rs.take()

    f0_take(0, (0,))
    f0_take(1, (0,))
    for k in (1, 2, 3):
        rs_end(k)

    for spread in bands: spread.sent()
    corners.sent()
    pl.when(r != 0)(f0rs.sent)
    for k in range(4):
        rs_sent(k)
    f0_sent()
    corner_sent()


def gather(jt, w0, w1, wrow, prior):
    dma = pltpu.SemaphoreType.DMA
    return pl.pallas_call(
        gather_kernel,
        out_shape=[
            jax.ShapeDtypeStruct((2, 512, 512), F32),
            jax.ShapeDtypeStruct((2, 512, 512), BF16),
            jax.ShapeDtypeStruct((512, 512), BF16),
            jax.ShapeDtypeStruct((4, 128, 512), F32),
            jax.ShapeDtypeStruct((512, 512), F32),
        ],
        in_specs=[VMEM] * 5,
        out_specs=[VMEM] * 5,
        scratch_shapes=[
            pltpu.VMEM((4, 4, 512, 512), BF16),
            pltpu.VMEM((4, 2, 512, 512), BF16),
            pltpu.VMEM((4, 2, 512, 512), BF16),
            pltpu.VMEM((2, 2, 2, 512, 512), BF16),
            pltpu.VMEM((2, 512, 512), F32),
            pltpu.VMEM((4, 128, 512), F32),
            pltpu.VMEM((4, 128, 512), F32),
            pltpu.VMEM((8, 512), F32),
            pltpu.VMEM((4, 8, 512), F32),
            dma((4, 3, 4, NCH)), dma((4, 4, NCH)), dma((4, 4)), dma((4, 4)),
            dma((3, 4, NC)), dma((4, NC)), dma((4,)), dma((4,)),
            dma((3, 4, NR)), dma((4, NR)), dma((4,)), dma((4,)),
            dma((4, 2)), dma((4, 2)), dma((2, 2, 2)), dma((2, 2)), dma((2,)),
            dma((2, 3)), dma((2, 4)), dma, dma((4,)),
        ],
        compiler_params=pltpu.CompilerParams(
            collective_id=0, has_side_effects=True, vmem_limit_bytes=58 * 2**20
        ),
        cost_estimate=pl.CostEstimate(flops=2 * 2048 * 2048 * 1024, bytes_accessed=2**24, transcendentals=0),
    )(jt, w0, w1, wrow, prior)


def split3(x):
    a = x.astype(BF16)
    rest = x - a.astype(F32)
    b = rest.astype(BF16)
    return a, b, (rest - b.astype(F32)).astype(BF16)


def invert_tile(m, size=16, beside=None):
    lane = lax.broadcasted_iota(jnp.int32, (size, 128), 1)
    row = lax.broadcasted_iota(jnp.int32, (size, 128), 0)
    rows = lax.broadcasted_iota(jnp.int32, (128, 128), 0)
    lanes = lax.broadcasted_iota(jnp.int32, (128, 128), 1)
    spread = lambda v: jnp.broadcast_to(v, (size, 128))

    def panel(p, m):
        if beside is not None:
            beside(p)
        active = 128 - size * p
        x = m[:size]
        cols = [spread(x[:, j:j + 1]) for j in range(size)]
        pivots = jnp.zeros((size, 128), F32)
        d = spread(cols[0][0:1])
        for j in range(size):
            q = pl.reciprocal(d, approx=True)
            q = q * (2.0 - d * q)
            pivots = jnp.where(row == j, d, pivots)
            below = jnp.where(row > j, cols[j], 0.0)
            if j + 1 < size:
                d = spread(cols[j + 1][j + 1:j + 2]) - q * (
                    spread(cols[j][j + 1:j + 2]) * spread(cols[j + 1][j:j + 1])
                )
            u = spread(jnp.where(lane[:1] == j, 1.0, x[j:j + 1]))
            x = jnp.where((lane == j) & (row >= j), jnp.where(row == j, 1.0, 0.0), x)
            x = x - q * (below * u)
            for k in range(j + 1, size):
                cols[k] = cols[k] - q * (below * spread(cols[k][j:j + 1]))
        s = lax.rsqrt(pivots)
        x = x * (s * (1.5 - 0.5 * pivots * s * s))
        x = jnp.where((lane < size) & (lane > row), 0.0, x)
        left = jnp.where((lane >= size) & (lane < active), x, 0.0)
        x1, x2, x3 = split3(x)
        y1, y2, y3 = split3(left)
        update = dotp(
            jnp.concatenate([y1, y1, y2, y2, y1, y3], axis=0),
            jnp.concatenate([x1, x2, x1, x2, x3, x1], axis=0), 0, 0,
        )
        m = jnp.where((lanes < size) & (rows < active), 0.0, m) - update
        m = jnp.concatenate([m[size:], x], axis=0)
        return pltpu.roll(m, 128 - size, 1)

    m = lax.fori_loop(0, 128 // size, panel, m)
    return jnp.where(rows >= lanes, m, 0.0)


def invert_step(a, j, beside=None):
    here = slice(128 * j, 128 * (j + 1))
    t = invert_tile(a[here, here], beside=beside)
    a[here, here] = t
    if j > 0:
        a[here, 0:128 * j] = dotp(t, a[here, 0:128 * j], precision=HIGHEST)
    if j < 3:
        low = 128 * (j + 1)
        a[here, low:] = dotp(t, a[here, low:], precision=HIGHEST)
        u = a[here, :]
        lanes = lax.broadcasted_iota(jnp.int32, (512 - low, 512), 1)
        kept = jnp.where((lanes >= 128 * j) & (lanes < low), 0.0, a[low:, :])
        a[low:, :] = kept - dotp(u[:, low:], u, 0, 0, precision=HIGHEST)
    else:
        rows = lax.broadcasted_iota(jnp.int32, (512, 512), 0)
        lanes = lax.broadcasted_iota(jnp.int32, (512, 512), 1)
        a[...] = jnp.where(rows >= lanes, a[...], 0.0)


def dot3(a, b, ca=1, cb=0):
    return dotp(a[0], b[0], ca, cb) + (dotp(a[0], b[1], ca, cb) + dotp(a[1], b[0], ca, cb))


def pair(x):
    a = x.astype(BF16)
    return a, (x - a.astype(F32)).astype(BF16)


def finish_kernel(f, f0, f0r, corner, inverse, out, res, sem):
    r, c = lax.axis_index("row"), lax.axis_index("col")
    linv = pair(inverse[...])

    def put(half):
        return pltpu.make_async_copy(res.at[half], out.at[:, half, :], sem.at[half])

    def panel(half):
        return dotp(linv[0], f0[half]) + dotp(linv[1], f0[half])

    @pl.when(r == 0)
    def _():
        @pl.when(c == 0)
        def _():
            res[0] = dot3(linv, pair(corner[...].reshape(512, 512)))

        @pl.when(c != 0)
        def _():
            res[0] = panel(0)
        put(0).start()
        res[1] = panel(1)
        put(1).start()

    @pl.when(r != 0)
    def _():
        right = pair(dotp(linv[0], f0r[...]) + dotp(linv[1], f0r[...]))

        @pl.when(c == 0)
        def _():
            res[0] = f[0]

        @pl.when(c != 0)
        def _():
            res[0] = f[0] - dot3(right, pair(panel(0)), 0, 0)
        put(0).start()
        res[1] = f[1] - dot3(right, pair(panel(1)), 0, 0)
        put(1).start()

    for half in (0, 1):
        put(half).wait()


def finish(f, f0, f0r, corner, inverse):
    return pl.pallas_call(
        finish_kernel,
        out_shape=jax.ShapeDtypeStruct((512, 2, 512), F32),
        in_specs=[VMEM] * 5,
        out_specs=pl.BlockSpec(memory_space=pl.ANY),
        scratch_shapes=[
            pltpu.VMEM((2, 512, 512), F32),
            pltpu.SemaphoreType.DMA((2,)),
        ],
        compiler_params=pltpu.CompilerParams(vmem_limit_bytes=56 * 2**20),
        cost_estimate=pl.CostEstimate(flops=2**31, bytes_accessed=2**23, transcendentals=0),
    )(f, f0, f0r, corner, inverse)


def body(sensitivity, sample_weight, pattern, prior):
    blocks = pattern.shape[0]
    x = sensitivity.reshape(blocks * 512, 1024)
    mask = jnp.repeat(pattern[:, :, 0].astype(F32), 512, axis=0)
    scale = sample_weight[:, None] * mask
    w = [
        (scale[:, i:i + 1] * x[:, 512 * i:512 * (i + 1)].astype(F32)).astype(BF16).reshape(blocks, 512, 512)
        for i in (0, 1)
    ]
    jt = (x[:, :512] * mask[:, 0:1].astype(BF16)).reshape(blocks, 512, 512).transpose(0, 2, 1)
    f, f0, f0r, corner, inverse = gather(
        jt, w[0], w[1], sample_weight.reshape(blocks, 1, 512), prior.reshape(1, 512)
    )
    return finish(f, f0, f0r, corner, inverse)


def solution(mesh):
    return jax.shard_map(
        body,
        mesh=mesh,
        in_specs=(P("row", None, "col"), P("row"), P("row", None, "col"), P("row")),
        out_specs=P("row", None, "col"),
        check_vma=False,
    )
```

```python
import jax
import jax.numpy as jnp
from jax import lax
from jax.experimental import pallas as pl
from jax.experimental.pallas import tpu as pltpu
from jax.sharding import PartitionSpec as P

F32 = jnp.float32
BF16 = jnp.bfloat16
HIGHEST = lax.Precision.HIGHEST
MESH = pl.DeviceIdType.MESH
VMEM = pl.BlockSpec(memory_space=pltpu.VMEM)
NCH = 8
CH = 256 // NCH
SKEW = 4
TILES = (0, 2, 1, 3)
T = 4 * NCH + 5 * SKEW
SKEWR = 4
NC = 4
NR = 2
SEND = {
    0: {0: ((0, 3, "mid"), (1, 1, "mid")), 3: ((1, 3, "end"),), 1: ((0, 1, "end"),)},
    2: {0: ((0, 3, "mid"), (1, 1, "mid")), 3: ((1, 3, "end"),), 1: ((0, 1, "end"),)},
    1: {3: ((0, 1, "mid"), (1, 1, "mid")), 2: ((0, 3, "end"), (1, 3, "end"))},
    3: {1: ((0, 3, "mid"), (1, 3, "mid")), 2: ((0, 1, "end"), (1, 1, "end"))},
}
MID = {
    0: {3: ((0, 3),), 1: ((1, 1),)},
    2: {3: ((0, 3),), 1: ((1, 1),)},
    1: {0: ((0, 1), (1, 1))},
    3: {0: ((0, 3), (1, 3))},
}
OWNER = {0: 2, 1: 1, 2: 2, 3: 3}


def dotp(a, b, ca=1, cb=0, precision=None):
    return lax.dot_general(
        a, b, (((ca,), (cb,)), ((), ())), precision=precision, preferred_element_type=F32
    )


def loop(n, f, start=0):
    lax.fori_loop(start, n, lambda i, carry: (f(i), carry)[1], 0)


class Place:
    def __init__(self):
        self.row = lax.axis_index("row")
        self.col = lax.axis_index("col")
        self.core = self.col % 2
        self.y = (self.col // 2) % 4
        self.z = self.col // 8
        self.sib = (self.row, self.col + 1 - 2 * self.core)

    def at(self, z, y, core):
        return (self.row, (z * 4 + y) * 2 + core)

    def along(self, step):
        return ((self.row + step) % 4, self.col)


class Tree:
    def __init__(self, pos, q, sy, skew):
        dz, dy = pos.z, (pos.y - sy + 4) % 4
        mz, my = (4 - dz) % 4, (4 - dy) % 4
        u, v = ((dz, dy), (dy, mz), (mz, my), (my, dz))[q]
        fwd = ((0, 1), (3, 0), (0, 3), (1, 0))[q]
        side = ((1, 0), (0, 1), (3, 0), (0, 3))[q]
        back = tuple((4 - d) % 4 for d in fwd)
        other = tuple((4 - d) % 4 for d in side)
        to = lambda d: pos.at((pos.z + d[0]) % 4, (pos.y + d[1]) % 4, pos.core)
        self.at_source = (dz == 0) & (dy == 0)
        depth = jnp.where(u == 0, v, 2 + jnp.where(u == 2, 1, 0) + jnp.where(v == 0, 1, v - 1))
        self.start = jnp.where(self.at_source, -1000, skew * depth)
        ahead = ((u == 0) & (v < 3)) | ((u >= 1) & ((v == 1) | (v == 2)))
        turn = tuple(jnp.where(u == 0, a, b) for a, b in zip(side, back))
        self.children = (
            (ahead, to(fwd)),
            (v == 1, to(turn)),
            ((v == 1) & ((u == 0) | (u == 3)), to(other)),
        )


class Spread:
    def __init__(self, pos, sy, column, n, src, dst, send, recv, sib_send, sib_recv, skew=SKEW):
        self.pos, self.n, self.sy = pos, n, sy
        self.trees = [Tree(pos, q, sy, skew) for q in range(4)]
        self.src, self.dst, self.send, self.recv = src, dst, send, recv
        self.sib_send, self.sib_recv = sib_send, sib_recv
        self.mine = pos.col == column
        self.first = pos.core * n

    def children(self, q, i):
        part = self.dst(q, self.first + i, 1)
        return [
            (pred, pltpu.make_async_remote_copy(
                part, part, self.send.at[k, q, i], self.recv.at[q, i],
                device_id=to, device_id_type=MESH))
            for k, (pred, to) in enumerate(self.trees[q].children)
        ]

    def root(self, q, h, i):
        step = ((0, 1), (3, 0), (0, 3), (1, 0))[q]
        j = h * self.n + i
        return pltpu.make_async_remote_copy(
            self.src(q, j, 1), self.dst(q, j, 1), self.send.at[h, q, i], self.recv.at[q, i],
            device_id=self.pos.at(step[0], (self.sy + step[1]) % 4, h), device_id_type=MESH)

    def sibling(self, q, ref, first, m):
        return pltpu.make_async_remote_copy(
            ref(q, first, m), self.dst(q, first, m), self.sib_send.at[q], self.sib_recv.at[q],
            device_id=self.pos.sib, device_id_type=MESH)

    def whole(self, q):
        return self.sibling(q, self.src, 0, 2 * self.n)

    def half(self, q):
        return self.sibling(q, self.dst, self.first, self.n)

    def begin(self, t):
        @pl.when(self.mine & (t >= 0) & (t < self.n))
        def _():
            for q in range(4):
                for h in (0, 1):
                    self.root(q, h, t).start()

            @pl.when(t == self.n - 1)
            def _():
                for q in range(4):
                    self.whole(q).start()

    def slot(self, t):
        self.begin(t)
        for q in range(4):
            i = t - self.trees[q].start

            @pl.when((i >= 0) & (i < self.n))
            def _():
                copies = self.children(q, i)
                copies[0][1].wait_recv()
                for pred, copy in copies:
                    pl.when(pred)(copy.start)
                pl.when(i == self.n - 1)(lambda: self.half(q).start())

    def take(self):
        at_source = self.trees[0].at_source
        for q in range(4):
            pl.when(jnp.logical_not(at_source))(
                self.sibling(q, self.dst, self.n - self.first, self.n).wait_recv)
            pl.when(at_source & jnp.logical_not(self.mine))(
                self.sibling(q, self.dst, 0, 2 * self.n).wait_recv)

    def sent(self):
        @pl.when(self.mine)
        def _():
            for q in range(4):
                def one(i):
                    for h in (0, 1):
                        self.root(q, h, i).wait_send()
                loop(self.n, one)
                self.whole(q).wait_send()

        @pl.when(jnp.logical_not(self.trees[0].at_source))
        def _():
            for q in range(4):
                def one(i):
                    for pred, copy in self.children(q, i):
                        pl.when(pred)(copy.wait_send)
                loop(self.n, one)
                self.half(q).wait_send()


def gather_kernel(
    jt, w0, w1, wrow, prior, f_out, f0_out, f0r_out, corner, linv,
    band, pb, rxm, rxd, f0acc, cpart, crx, dg, dgr,
    b_send, b_recv, bs_send, bs_recv, c_send, c_recv, cs_send, cs_recv,
    r_send, r_recv, rs_send2, rs_recv2,
    rs_sem, rxm_sem, rxd_sem, f0_send, f0_recv, cx_send, cx_recv, dg_send, dg_recv,
):
    pos = Place()
    r, c = pos.row, pos.col

    near, far = c < 4, c >= 4
    barrier = pltpu.get_barrier_semaphore()
    greet = [pos.sib, pos.along(1), pos.along(2), pos.along(3)]
    for core in (0, 1):
        for step in (1, 3):
            greet.append(pos.at((pos.z + step) % 4, pos.y, core))
            greet.append(pos.at(pos.z, (pos.y + step) % 4, core))
    for to in greet:
        pl.semaphore_signal(barrier, inc=1, device_id=to, device_id_type=MESH)
    pl.semaphore_wait(barrier, len(greet))

    def run(i, m, rows):
        return pl.ds(pl.multiple_of(i * rows, rows), m * rows)

    bands = []
    for n, tile in enumerate(TILES):
        bands.append(Spread(
            pos, tile // 2, tile, NCH,
            lambda q, i, m: jt.at[q, run(i, m, CH)],
            lambda q, i, m, n=n: band.at[q, n, run(i, m, CH)],
            b_send.at[n], b_recv.at[n], bs_send.at[n], bs_recv.at[n]))

    def corner_rows(q, i, m):
        return corner.at[q, run(i, m, 64 // NC)]

    corners = Spread(pos, 0, 0, NC, corner_rows, corner_rows, c_send, c_recv, cs_send, cs_recv)

    def f0r_rows(ref):
        rows = 64 // NR
        return lambda q, i, m: ref.at[pl.ds(pl.multiple_of(q * 128 + i * rows, rows), m * rows)]

    f0rs = Spread(pos, r // 2, r, NR, f0r_rows(f0_out.at[0]), f0r_rows(f0r_out),
                  r_send, r_recv, rs_send2, rs_recv2, SKEWR)

    def band_slot(t):
        for n in range(4):
            @pl.when((t >= NCH * n) & (t < NCH * (n + 1) + 5 * SKEW))
            def _():
                bands[n].slot(t - NCH * n)

    def corner_slot(t):
        corners.slot(t)

    def f0r_slot(t):
        f0rs.slot(t)

    def own_tile():
        for n, tile in enumerate(TILES):
            @pl.when(c == tile)
            def _():
                for q in range(4):
                    band[q, n] = jt[q]

    def corner_x(dst, src, i, kind, frm):
        return pltpu.make_async_remote_copy(
            src, dst, cx_send.at[kind, i - 1], cx_recv.at[kind, frm],
            device_id=pos.along(i), device_id_type=MESH,
        )

    def corner_part():
        @pl.when(c == 0)
        def _():
            a = lax.broadcasted_iota(jnp.int32, (128, 512), 0)
            b = lax.broadcasted_iota(jnp.int32, (128, 512), 1)
            for i in range(4):
                acc = jnp.where((b == a + 128 * i) & (r == 0), prior[...], 0.0)
                for q in range(4):
                    acc += dotp(jt[q, 128 * i:128 * (i + 1), :], w0[q])
                cpart[i] = acc
            for i in (1, 2, 3):
                corner_x(crx.at[r], cpart.at[(r + i) % 4], i, 0, r).start()

    def corner_sum():
        @pl.when(c == 0)
        def _():
            total = cpart[r]
            for i in (1, 2, 3):
                frm = (r + i) % 4
                corner_x(crx.at[frm], crx.at[frm], i, 0, frm).wait_recv()
                total += crx[frm]
            corner[r] = total
            for i in (1, 2, 3):
                corner_x(corner.at[r], corner.at[r], i, 1, r).start()

    def corner_take():
        @pl.when(c == 0)
        def _():
            for i in (1, 2, 3):
                frm = (r + i) % 4
                corner_x(corner.at[frm], corner.at[frm], i, 1, frm).wait_recv()

    def corner_sent():
        @pl.when(c == 0)
        def _():
            for i in (1, 2, 3):
                corner_x(crx.at[r], cpart.at[(r + i) % 4], i, 0, r).wait_send()
                corner_x(corner.at[r], corner.at[r], i, 1, r).wait_send()

    def f0r_own():
        @pl.when(c == r)
        def _():
            f0r_out[...] = f0_out[0]

    def tile_of(k, q):
        return band[q, TILES.index(k)]

    def piece(k, half, n):
        cols = pl.ds(pl.multiple_of(n * 256, 256), 256)
        w = (w0, w1)[half]
        acc = dotp(tile_of(k, 0), w[0, :, cols])
        for q in range(1, 4):
            acc += dotp(tile_of(k, q), w[q, :, cols])
        own = r == OWNER[k]

        def put(value):
            @pl.when(own)
            def _():
                if k == 0:
                    f0acc[half, :, cols] = value
                else:
                    f_out[half, :, cols] = value

            @pl.when(jnp.logical_not(own))
            def _():
                pb[k, half, :, cols] = value.astype(BF16)

        if k == 0 or half == 1:
            put(acc)
            return

        @pl.when(c == 0)
        def _():
            value = acc
            first = pl.ds(pl.multiple_of(n * 256, 256), 256)
            for q in range(4):
                wk = (tile_of(k, q).astype(F32) * wrow[q]).astype(BF16)
                value = value - dotp(wk, band[q, 0, first], 1, 1)
            put(value)

        @pl.when(c == k)
        def _():
            a = lax.broadcasted_iota(jnp.int32, (512, 256), 0)
            b = lax.broadcasted_iota(jnp.int32, (512, 256), 1)
            on = a == b + n * 256
            line = jnp.sum(jnp.where(on, acc, 0.0), axis=0, keepdims=True)
            dg[:, cols] = jnp.broadcast_to(line, (8, 256))
            put(jnp.where(on, 0.0, acc))

        pl.when((c != 0) & (c != k))(lambda: put(acc))

    def dg_copy(i, frm):
        return pltpu.make_async_remote_copy(
            dg, dgr.at[frm], dg_send, dg_recv.at[frm], device_id=pos.along(i), device_id_type=MESH
        )

    def move(k, half, step, kind):
        e = 0 if k == 0 else 1
        side = 0 if step == 3 else 1
        dst, sem = (
            (rxm.at[k, half], rxm_sem.at[k, half]) if kind == "mid"
            else (rxd.at[e, side, half], rxd_sem.at[e, side, half])
        )
        return pltpu.make_async_remote_copy(
            pb.at[k, half], dst, rs_sem.at[k, half], sem, device_id=pos.along(step), device_id_type=MESH
        )

    def rs_send(k):
        for row, moves in SEND[k].items():
            @pl.when(r == row)
            def _():
                for m in moves:
                    move(k, *m).start()
        if k:
            for i in (1, 2, 3):
                pl.when((c == k) & ((r + i) % 4 == k))(dg_copy(i, r).start)

    def rs_mid(k):
        for row, moves in MID[k].items():
            @pl.when(r == row)
            def _():
                for half, step in moves:
                    move(k, half, step, "mid").wait_recv()
                    pb[k, half] = (pb[k, half].astype(F32) + rxm[k, half].astype(F32)).astype(BF16)
                    move(k, half, step, "end").start()

    def rs_end(k):
        e = 0 if k == 0 else 1

        @pl.when(r == OWNER[k])
        def _():
            for half in (0, 1):
                for step in (1, 3):
                    move(k, half, step, "end").wait_recv()
                got = rxd[e, 0, half].astype(F32) + rxd[e, 1, half].astype(F32)
                if k == 0:
                    f0_out[half] = (f0acc[half] + got).astype(BF16)
                else:
                    f_out[half] = f_out[half] + got
            if k == 0:
                f0_copy(0, 3).start()
                f0_copy(1, 1).start()
                pl.when(near)(f0_rest)
            if k == 0:
                return

            @pl.when(c == k)
            def _():
                line = prior[...]
                for i in (1, 2, 3):
                    frm = (r + i) % 4
                    dg_copy(i, frm).wait_recv()
                    line = line + dgr[frm, 0:1, :]
                a = lax.broadcasted_iota(jnp.int32, (512, 512), 0)
                b = lax.broadcasted_iota(jnp.int32, (512, 512), 1)
                own = jnp.sum(jnp.where(a == b, f_out[0], 0.0), axis=0, keepdims=True)
                own = own + dg[0:1, :]
                f_out[0] = jnp.where(a == b, own + line, f_out[0])

    def rs_sent(k):
        for table in (SEND, MID):
            for row, moves in table[k].items():
                @pl.when(r == row)
                def _():
                    for m in moves:
                        move(k, m[0], m[1], "end").wait_send()
        if k:
            for i in (1, 2, 3):
                pl.when((c == k) & ((r + i) % 4 == k))(dg_copy(i, r).wait_send)

    def f0_copy(half, step):
        return pltpu.make_async_remote_copy(
            f0_out.at[half], f0_out.at[half], f0_send.at[half, step // 2], f0_recv.at[half],
            device_id=pos.along(step), device_id_type=MESH,
        )

    def f0_rest():
        f0_copy(0, 1).start()
        f0_copy(1, 3).start()

    def f0_take(half, rows):
        for row in rows:
            pl.when(r == row)(f0_copy(half, 1).wait_recv)
        if half == 0:
            if 1 in rows: pl.when(r == 1)(f0_copy(0, 3).start)
        elif 3 in rows:
            pl.when(r == 3)(f0_copy(1, 1).start)

    def f0_sent():
        @pl.when(r == 2)
        def _():
            for half in (0, 1):
                for step in (1, 3):
                    f0_copy(half, step).wait_send()
        pl.when(r == 1)(f0_copy(0, 3).wait_send)
        pl.when(r == 3)(f0_copy(1, 1).wait_send)

    C0 = 20

    def both(t):
        band_slot(t)
        pl.when((t >= C0) & (t < C0 + NC + 5 * SKEW))(lambda: corner_slot(t - C0))

    def slots(a, b):
        loop(b, both, a)

    def product(k, t=None):
        bands[TILES.index(k)].take()
        for half in (0, 1):
            def one(n):
                piece(k, half, n)
                if t is not None: both(t + 2 * half + n)
            loop(2, one)

    P0 = NCH + 5 * SKEW

    def first_product():
        product(0)
        rs_send(0)

    slots(0, 2)
    corner_part()
    slots(2, 12)
    own_tile()
    corner_sum()
    slots(12, C0)
    corner_take()
    slots(C0, 22)
    pl.when(near)(first_product)
    slots(22, P0 + 1)
    pl.when(far)(first_product)
    slots(P0 + 1, P0 + NCH + 1)
    product(2, P0 + NCH + 1)
    rs_send(2)
    pl.when(near)(lambda: rs_mid(0))
    slots(P0 + NCH + 5, P0 + 2 * NCH + 1)
    product(1, P0 + 2 * NCH + 1)
    rs_send(1)
    pl.when(far)(lambda: rs_mid(0))
    slots(P0 + 2 * NCH + 5, T)
    pl.when(near)(lambda: rs_end(0))
    product(3)
    rs_send(3)
    rs_mid(2)
    corners.take()
    for q in range(4):
        linv[128 * q:128 * (q + 1), :] = corner[q]
    beside = lambda j: lambda p: pl.when(r != 0)(lambda: f0r_slot(p + 8 * j))
    invert_step(linv, 0)
    rs_mid(1)
    pl.when(far)(lambda: rs_end(0))
    rs_mid(3)
    pl.when(near)(lambda: f0_take(0, (1, 3)))
    invert_step(linv, 1, beside(0))
    pl.when(far & (r == 2))(f0_rest)
    invert_step(linv, 2, beside(1))
    pl.when(r != 0)(lambda: loop(NR + 5 * SKEWR, f0r_slot, 16))
    f0_take(1, (3,))
    pl.when(far)(lambda: f0_take(0, (1,)))
    invert_step(linv, 3)
    f0_take(1, (1,))
    pl.when(far)(lambda: f0_take(0, (3,)))

    @pl.when(r != 0)
    def _():
        f0r_own()
        f0rs.take()

    f0_take(0, (0,))
    f0_take(1, (0,))
    for k in (1, 2, 3):
        rs_end(k)

    for spread in bands: spread.sent()
    corners.sent()
    pl.when(r != 0)(f0rs.sent)
    for k in range(4):
        rs_sent(k)
    f0_sent()
    corner_sent()


def gather(jt, w0, w1, wrow, prior):
    dma = pltpu.SemaphoreType.DMA
    return pl.pallas_call(
        gather_kernel,
        out_shape=[
            jax.ShapeDtypeStruct((2, 512, 512), F32),
            jax.ShapeDtypeStruct((2, 512, 512), BF16),
            jax.ShapeDtypeStruct((512, 512), BF16),
            jax.ShapeDtypeStruct((4, 128, 512), F32),
            jax.ShapeDtypeStruct((512, 512), F32),
        ],
        in_specs=[VMEM] * 5,
        out_specs=[VMEM] * 5,
        scratch_shapes=[
            pltpu.VMEM((4, 4, 512, 512), BF16),
            pltpu.VMEM((4, 2, 512, 512), BF16),
            pltpu.VMEM((4, 2, 512, 512), BF16),
            pltpu.VMEM((2, 2, 2, 512, 512), BF16),
            pltpu.VMEM((2, 512, 512), F32),
            pltpu.VMEM((4, 128, 512), F32),
            pltpu.VMEM((4, 128, 512), F32),
            pltpu.VMEM((8, 512), F32),
            pltpu.VMEM((4, 8, 512), F32),
            dma((4, 3, 4, NCH)), dma((4, 4, NCH)), dma((4, 4)), dma((4, 4)),
            dma((3, 4, NC)), dma((4, NC)), dma((4,)), dma((4,)),
            dma((3, 4, NR)), dma((4, NR)), dma((4,)), dma((4,)),
            dma((4, 2)), dma((4, 2)), dma((2, 2, 2)), dma((2, 2)), dma((2,)),
            dma((2, 3)), dma((2, 4)), dma, dma((4,)),
        ],
        compiler_params=pltpu.CompilerParams(
            collective_id=0, has_side_effects=True, vmem_limit_bytes=58 * 2**20
        ),
        cost_estimate=pl.CostEstimate(flops=2 * 2048 * 2048 * 1024, bytes_accessed=2**24, transcendentals=0),
    )(jt, w0, w1, wrow, prior)


def split3(x):
    a = x.astype(BF16)
    rest = x - a.astype(F32)
    b = rest.astype(BF16)
    return a, b, (rest - b.astype(F32)).astype(BF16)


def invert_tile(m, size=16, beside=None):
    lane = lax.broadcasted_iota(jnp.int32, (size, 128), 1)
    row = lax.broadcasted_iota(jnp.int32, (size, 128), 0)
    rows = lax.broadcasted_iota(jnp.int32, (128, 128), 0)
    lanes = lax.broadcasted_iota(jnp.int32, (128, 128), 1)
    spread = lambda v: jnp.broadcast_to(v, (size, 128))

    def panel(p, m):
        if beside is not None:
            beside(p)
        active = 128 - size * p
        x = m[:size]
        cols = [spread(x[:, j:j + 1]) for j in range(size)]
        pivots = jnp.zeros((size, 128), F32)
        d = spread(cols[0][0:1])
        for j in range(size):
            q = pl.reciprocal(d, approx=True)
            q = q * (2.0 - d * q)
            pivots = jnp.where(row == j, d, pivots)
            below = jnp.where(row > j, cols[j], 0.0)
            if j + 1 < size:
                d = spread(cols[j + 1][j + 1:j + 2]) - q * (
                    spread(cols[j][j + 1:j + 2]) * spread(cols[j + 1][j:j + 1])
                )
            u = spread(jnp.where(lane[:1] == j, 1.0, x[j:j + 1]))
            x = jnp.where((lane == j) & (row >= j), jnp.where(row == j, 1.0, 0.0), x)
            x = x - q * (below * u)
            for k in range(j + 1, size):
                cols[k] = cols[k] - q * (below * spread(cols[k][j:j + 1]))
        s = lax.rsqrt(pivots)
        x = x * (s * (1.5 - 0.5 * pivots * s * s))
        x = jnp.where((lane < size) & (lane > row), 0.0, x)
        left = jnp.where((lane >= size) & (lane < active), x, 0.0)
        x1, x2, x3 = split3(x)
        y1, y2, y3 = split3(left)
        update = dotp(
            jnp.concatenate([y1, y1, y2, y2, y1, y3], axis=0),
            jnp.concatenate([x1, x2, x1, x2, x3, x1], axis=0), 0, 0,
        )
        m = jnp.where((lanes < size) & (rows < active), 0.0, m) - update
        m = jnp.concatenate([m[size:], x], axis=0)
        return pltpu.roll(m, 128 - size, 1)

    m = lax.fori_loop(0, 128 // size, panel, m)
    return jnp.where(rows >= lanes, m, 0.0)


def invert_step(a, j, beside=None):
    here = slice(128 * j, 128 * (j + 1))
    t = invert_tile(a[here, here], beside=beside)
    a[here, here] = t
    if j > 0:
        a[here, 0:128 * j] = dotp(t, a[here, 0:128 * j], precision=HIGHEST)
    if j < 3:
        low = 128 * (j + 1)
        a[here, low:] = dotp(t, a[here, low:], precision=HIGHEST)
        u = a[here, :]
        lanes = lax.broadcasted_iota(jnp.int32, (512 - low, 512), 1)
        kept = jnp.where((lanes >= 128 * j) & (lanes < low), 0.0, a[low:, :])
        a[low:, :] = kept - dotp(u[:, low:], u, 0, 0, precision=HIGHEST)
    else:
        rows = lax.broadcasted_iota(jnp.int32, (512, 512), 0)
        lanes = lax.broadcasted_iota(jnp.int32, (512, 512), 1)
        a[...] = jnp.where(rows >= lanes, a[...], 0.0)


def dot3(a, b, ca=1, cb=0):
    return dotp(a[0], b[0], ca, cb) + (dotp(a[0], b[1], ca, cb) + dotp(a[1], b[0], ca, cb))


def pair(x):
    a = x.astype(BF16)
    return a, (x - a.astype(F32)).astype(BF16)


def finish_kernel(f, f0, f0r, corner, inverse, out, res, sem):
    r, c = lax.axis_index("row"), lax.axis_index("col")
    linv = pair(inverse[...])

    def put(half):
        return pltpu.make_async_copy(res.at[half], out.at[:, half, :], sem.at[half])

    def panel(half):
        return dotp(linv[0], f0[half]) + dotp(linv[1], f0[half])

    @pl.when(r == 0)
    def _():
        @pl.when(c == 0)
        def _():
            res[0] = dot3(linv, pair(corner[...].reshape(512, 512)))

        @pl.when(c != 0)
        def _():
            res[0] = panel(0)
        put(0).start()
        res[1] = panel(1)
        put(1).start()

    @pl.when(r != 0)
    def _():
        right = pair(dotp(linv[0], f0r[...]) + dotp(linv[1], f0r[...]))

        @pl.when(c == 0)
        def _():
            res[0] = f[0]

        @pl.when(c != 0)
        def _():
            res[0] = f[0] - dot3(right, pair(panel(0)), 0, 0)
        put(0).start()
        res[1] = f[1] - dot3(right, pair(panel(1)), 0, 0)
        put(1).start()

    for half in (0, 1):
        put(half).wait()


def finish(f, f0, f0r, corner, inverse):
    return pl.pallas_call(
        finish_kernel,
        out_shape=jax.ShapeDtypeStruct((512, 2, 512), F32),
        in_specs=[VMEM] * 5,
        out_specs=pl.BlockSpec(memory_space=pl.ANY),
        scratch_shapes=[
            pltpu.VMEM((2, 512, 512), F32),
            pltpu.SemaphoreType.DMA((2,)),
        ],
        compiler_params=pltpu.CompilerParams(vmem_limit_bytes=56 * 2**20),
        cost_estimate=pl.CostEstimate(flops=2**31, bytes_accessed=2**23, transcendentals=0),
    )(f, f0, f0r, corner, inverse)


def body(sensitivity, sample_weight, pattern, prior):
    blocks = pattern.shape[0]
    x = sensitivity.reshape(blocks * 512, 1024)
    mask = jnp.repeat(pattern[:, :, 0].astype(F32), 512, axis=0)
    scale = sample_weight[:, None] * mask
    w = [
        (scale[:, i:i + 1] * x[:, 512 * i:512 * (i + 1)].astype(F32)).astype(BF16).reshape(blocks, 512, 512)
        for i in (0, 1)
    ]
    jt = (x[:, :512] * mask[:, 0:1].astype(BF16)).reshape(blocks, 512, 512).transpose(0, 2, 1)
    f, f0, f0r, corner, inverse = gather(
        jt, w[0], w[1], sample_weight.reshape(blocks, 1, 512), prior.reshape(1, 512)
    )
    return finish(f, f0, f0r, corner, inverse)


def solution(mesh):
    return jax.shard_map(
        body,
        mesh=mesh,
        in_specs=(P("row", None, "col"), P("row"), P("row", None, "col"), P("row")),
        out_specs=P("row", None, "col"),
        check_vma=False,
    )
```

```python
import jax
import jax.numpy as jnp
from jax import lax
from jax.experimental import pallas as pl
from jax.experimental.pallas import tpu as pltpu
from jax.sharding import PartitionSpec as P

F32 = jnp.float32
BF16 = jnp.bfloat16
HIGHEST = lax.Precision.HIGHEST
MESH = pl.DeviceIdType.MESH
VMEM = pl.BlockSpec(memory_space=pltpu.VMEM)
NCH = 8
CH = 512 // NCH
SKEW = 4
TILES = (0, 2, 1, 3)
T = 4 * NCH + 5 * SKEW
SKEWR = 4
NC = 4
NR = 2
SEND = {
    0: {0: ((0, 3, "mid"), (1, 1, "mid")), 3: ((1, 3, "end"),), 1: ((0, 1, "end"),)},
    2: {0: ((0, 3, "mid"), (1, 1, "mid")), 3: ((1, 3, "end"),), 1: ((0, 1, "end"),)},
    1: {3: ((0, 1, "mid"), (1, 1, "mid")), 2: ((0, 3, "end"), (1, 3, "end"))},
    3: {1: ((0, 3, "mid"), (1, 3, "mid")), 2: ((0, 1, "end"), (1, 1, "end"))},
}
MID = {
    0: {3: ((0, 3),), 1: ((1, 1),)},
    2: {3: ((0, 3),), 1: ((1, 1),)},
    1: {0: ((0, 1), (1, 1))},
    3: {0: ((0, 3), (1, 3))},
}
OWNER = {0: 2, 1: 1, 2: 2, 3: 3}


def dotp(a, b, ca=1, cb=0, precision=None):
    return lax.dot_general(
        a, b, (((ca,), (cb,)), ((), ())), precision=precision, preferred_element_type=F32
    )


def loop(n, f, start=0):
    lax.fori_loop(start, n, lambda i, carry: (f(i), carry)[1], 0)


class Place:
    def __init__(self):
        self.row = lax.axis_index("row")
        self.col = lax.axis_index("col")
        self.core = self.col % 2
        self.y = (self.col // 2) % 4
        self.z = self.col // 8
        self.sib = (self.row, self.col + 1 - 2 * self.core)

    def at(self, z, y, core):
        return (self.row, (z * 4 + y) * 2 + core)

    def along(self, step):
        return ((self.row + step) % 4, self.col)


class Tree:
    def __init__(self, pos, m, sy, skew):
        dz, dy = pos.z, (pos.y - sy + 4) % 4
        mz, my = (4 - dz) % 4, (4 - dy) % 4
        first = pos.core == 0
        pick = lambda table: tuple(
            jnp.where(first, a, b) for a, b in zip(table[m], table[2 + m])
        )
        u, v = pick(((dz, dy), (dy, mz), (mz, my), (my, dz)))
        fwd = pick(((0, 1), (3, 0), (0, 3), (1, 0)))
        side = pick(((1, 0), (0, 1), (3, 0), (0, 3)))
        back = tuple((4 - d) % 4 for d in fwd)
        other = tuple((4 - d) % 4 for d in side)
        to = lambda d: pos.at((pos.z + d[0]) % 4, (pos.y + d[1]) % 4, pos.core)
        self.q = 2 * pos.core + m
        self.at_source = (dz == 0) & (dy == 0)
        depth = jnp.where(u == 0, v, 2 + jnp.where(u == 2, 1, 0) + jnp.where(v == 0, 1, v - 1))
        self.start = jnp.where(self.at_source, -1000, skew * depth)
        ahead = ((u == 0) & (v < 3)) | ((u >= 1) & ((v == 1) | (v == 2)))
        turn = tuple(jnp.where(u == 0, a, b) for a, b in zip(side, back))
        self.children = (
            (ahead, to(fwd)),
            (v == 1, to(turn)),
            ((v == 1) & ((u == 0) | (u == 3)), to(other)),
        )


class Spread:
    def __init__(self, pos, sy, column, n, src, dst, send, recv, sib_send, sib_recv, skew=SKEW):
        self.pos, self.column, self.n = pos, column, n
        self.trees = [Tree(pos, m, sy, skew) for m in (0, 1)]
        self.dst, self.send, self.recv = dst, send, recv
        self.sib_send, self.sib_recv = sib_send, sib_recv
        self.src = src
        self.mine = pos.col == column
        self.sy = sy

    def children(self, tree, i):
        q = tree.q
        return [
            (pred, pltpu.make_async_remote_copy(
                self.dst(q, i, 1), self.dst(q, i, 1), self.send.at[k, q, i], self.recv.at[q, i],
                device_id=to, device_id_type=MESH))
            for k, (pred, to) in enumerate(tree.children)
        ]

    def root(self, q, i):
        step = ((0, 1), (3, 0), (0, 3), (1, 0))[q]
        pos = self.pos
        return pltpu.make_async_remote_copy(
            self.src(q, i, 1), self.dst(q, i, 1), self.send.at[0, q, i], self.recv.at[q, i],
            device_id=pos.at(step[0], (self.sy + step[1]) % 4, q // 2), device_id_type=MESH)

    def sibling(self, q, src):
        return pltpu.make_async_remote_copy(
            src(q, 0, self.n), self.dst(q, 0, self.n), self.sib_send.at[q], self.sib_recv.at[q],
            device_id=self.pos.sib, device_id_type=MESH)

    def begin(self, t):
        @pl.when(self.mine & (t >= 0) & (t < self.n))
        def _():
            for q in range(4):
                self.root(q, t).start()

            @pl.when(t == self.n - 1)
            def _():
                for q in range(4):
                    self.sibling(q, self.src).start()

    def slot(self, t):
        self.begin(t)
        for tree in self.trees:
            i = t - tree.start

            @pl.when((i >= 0) & (i < self.n))
            def _():
                copies = self.children(tree, i)
                copies[0][1].wait_recv()
                for pred, copy in copies:
                    pl.when(pred)(copy.start)
                pl.when(i == self.n - 1)(lambda: self.sibling(tree.q, self.dst).start())

    def take(self):
        away = jnp.logical_not(self.trees[0].at_source)
        other = 1 - self.pos.core
        for q in range(4):
            @pl.when((away & (other == q // 2)) | (self.trees[0].at_source & jnp.logical_not(self.mine)))
            def _():
                self.sibling(q, self.dst).wait_recv()

    def sent(self):
        @pl.when(self.mine)
        def _():
            for q in range(4):
                loop(self.n, lambda i: self.root(q, i).wait_send())
                self.sibling(q, self.src).wait_send()
        for tree in self.trees:
            @pl.when(jnp.logical_not(tree.at_source))
            def _():
                def one(i):
                    for pred, copy in self.children(tree, i):
                        pl.when(pred)(copy.wait_send)
                loop(self.n, one)
                self.sibling(tree.q, self.dst).wait_send()


def gather_kernel(
    jt, w0, w1, wrow, prior, f_out, f0_out, f0r_out, corner, linv,
    band, pb, rxm, rxd, f0acc, cpart, crx, dg, dgr,
    b_send, b_recv, bs_send, bs_recv, c_send, c_recv, cs_send, cs_recv,
    r_send, r_recv, rs_send2, rs_recv2,
    rs_sem, rxm_sem, rxd_sem, f0_send, f0_recv, cx_send, cx_recv, dg_send, dg_recv,
):
    pos = Place()
    r, c = pos.row, pos.col

    barrier = pltpu.get_barrier_semaphore()
    greet = [pos.sib, pos.along(1), pos.along(2), pos.along(3)]
    for core in (0, 1):
        for step in (1, 3):
            greet.append(pos.at((pos.z + step) % 4, pos.y, core))
            greet.append(pos.at(pos.z, (pos.y + step) % 4, core))
    for to in greet:
        pl.semaphore_signal(barrier, inc=1, device_id=to, device_id_type=MESH)
    pl.semaphore_wait(barrier, len(greet))

    def run(q, i, n, rows):
        return pl.ds(pl.multiple_of((q * 0 + i) * rows, rows), n * rows)

    bands = []
    for n, tile in enumerate(TILES):
        bands.append(Spread(
            pos, tile // 2, tile, NCH,
            lambda q, i, m: jt.at[q, run(q, i, m, CH)],
            lambda q, i, m, n=n: band.at[q, n, run(q, i, m, CH)],
            b_send.at[n], b_recv.at[n], bs_send.at[n], bs_recv.at[n]))

    def corner_rows(q, i, m):
        return corner.at[q, run(q, i, m, 128 // NC)]

    corners = Spread(pos, 0, 0, NC, corner_rows, corner_rows, c_send, c_recv, cs_send, cs_recv)

    def f0r_rows(ref):
        return lambda q, i, m: ref.at[pl.ds(
            pl.multiple_of(q * 128 + i * (128 // NR), 128 // NR), m * (128 // NR))]

    f0rs = Spread(pos, r // 2, r, NR, f0r_rows(f0_out.at[0]), f0r_rows(f0r_out),
                  r_send, r_recv, rs_send2, rs_recv2, SKEWR)

    def band_slot(t):
        for n in range(4):
            @pl.when((t >= NCH * n) & (t < NCH * (n + 1) + 5 * SKEW))
            def _():
                bands[n].slot(t - NCH * n)

    def corner_slot(t):
        corners.slot(t)

    def f0r_slot(t):
        f0rs.slot(t)

    def own_tile():
        for n, tile in enumerate(TILES):
            @pl.when(c == tile)
            def _():
                for q in range(4):
                    band[q, n] = jt[q]

    def corner_x(dst, src, i, kind, frm):
        return pltpu.make_async_remote_copy(
            src, dst, cx_send.at[kind, i - 1], cx_recv.at[kind, frm],
            device_id=pos.along(i), device_id_type=MESH,
        )

    def corner_part():
        @pl.when(c == 0)
        def _():
            a = lax.broadcasted_iota(jnp.int32, (128, 512), 0)
            b = lax.broadcasted_iota(jnp.int32, (128, 512), 1)
            for i in range(4):
                acc = jnp.where((b == a + 128 * i) & (r == 0), prior[...], 0.0)
                for q in range(4):
                    acc += dotp(jt[q, 128 * i:128 * (i + 1), :], w0[q])
                cpart[i] = acc
            for i in (1, 2, 3):
                corner_x(crx.at[r], cpart.at[(r + i) % 4], i, 0, r).start()

    def corner_sum():
        @pl.when(c == 0)
        def _():
            total = cpart[r]
            for i in (1, 2, 3):
                frm = (r + i) % 4
                corner_x(crx.at[frm], crx.at[frm], i, 0, frm).wait_recv()
                total += crx[frm]
            corner[r] = total
            for i in (1, 2, 3):
                corner_x(corner.at[r], corner.at[r], i, 1, r).start()

    def corner_take():
        @pl.when(c == 0)
        def _():
            for i in (1, 2, 3):
                frm = (r + i) % 4
                corner_x(corner.at[frm], corner.at[frm], i, 1, frm).wait_recv()

    def corner_sent():
        @pl.when(c == 0)
        def _():
            for i in (1, 2, 3):
                corner_x(crx.at[r], cpart.at[(r + i) % 4], i, 0, r).wait_send()
                corner_x(corner.at[r], corner.at[r], i, 1, r).wait_send()

    def f0r_own():
        @pl.when(c == r)
        def _():
            f0r_out[...] = f0_out[0]

    def tile_of(k, q):
        return band[q, TILES.index(k)]

    def piece(k, half, n):
        cols = pl.ds(pl.multiple_of(n * 256, 256), 256)
        w = (w0, w1)[half]
        acc = dotp(tile_of(k, 0), w[0, :, cols])
        for q in range(1, 4):
            acc += dotp(tile_of(k, q), w[q, :, cols])
        own = r == OWNER[k]

        def put(value):
            @pl.when(own)
            def _():
                if k == 0:
                    f0acc[half, :, cols] = value
                else:
                    f_out[half, :, cols] = value

            @pl.when(jnp.logical_not(own))
            def _():
                pb[k, half, :, cols] = value.astype(BF16)

        if k == 0 or half == 1:
            put(acc)
            return

        @pl.when(c == 0)
        def _():
            value = acc
            first = pl.ds(pl.multiple_of(n * 256, 256), 256)
            for q in range(4):
                wk = (tile_of(k, q).astype(F32) * wrow[q]).astype(BF16)
                value = value - dotp(wk, band[q, 0, first], 1, 1)
            put(value)

        @pl.when(c == k)
        def _():
            a = lax.broadcasted_iota(jnp.int32, (512, 256), 0)
            b = lax.broadcasted_iota(jnp.int32, (512, 256), 1)
            on = a == b + n * 256
            line = jnp.sum(jnp.where(on, acc, 0.0), axis=0, keepdims=True)
            dg[:, cols] = jnp.broadcast_to(line, (8, 256))
            put(jnp.where(on, 0.0, acc))

        pl.when((c != 0) & (c != k))(lambda: put(acc))

    def dg_copy(i, frm):
        return pltpu.make_async_remote_copy(
            dg, dgr.at[frm], dg_send, dg_recv.at[frm], device_id=pos.along(i), device_id_type=MESH
        )

    def move(k, half, step, kind):
        e = 0 if k == 0 else 1
        side = 0 if step == 3 else 1
        dst, sem = (
            (rxm.at[k, half], rxm_sem.at[k, half]) if kind == "mid"
            else (rxd.at[e, side, half], rxd_sem.at[e, side, half])
        )
        return pltpu.make_async_remote_copy(
            pb.at[k, half], dst, rs_sem.at[k, half], sem, device_id=pos.along(step), device_id_type=MESH
        )

    def rs_send(k):
        for row, moves in SEND[k].items():
            @pl.when(r == row)
            def _():
                for m in moves:
                    move(k, *m).start()
        if k:
            for i in (1, 2, 3):
                pl.when((c == k) & ((r + i) % 4 == k))(dg_copy(i, r).start)

    def rs_mid(k):
        for row, moves in MID[k].items():
            @pl.when(r == row)
            def _():
                for half, step in moves:
                    move(k, half, step, "mid").wait_recv()
                    pb[k, half] = (pb[k, half].astype(F32) + rxm[k, half].astype(F32)).astype(BF16)
                    move(k, half, step, "end").start()

    def rs_end(k):
        e = 0 if k == 0 else 1

        @pl.when(r == OWNER[k])
        def _():
            for half in (0, 1):
                for step in (1, 3):
                    move(k, half, step, "end").wait_recv()
                got = rxd[e, 0, half].astype(F32) + rxd[e, 1, half].astype(F32)
                if k == 0:
                    f0_out[half] = (f0acc[half] + got).astype(BF16)
                    for step in (1, 3):
                        f0_copy(half, step).start()
                else:
                    f_out[half] = f_out[half] + got
            if k == 0:
                return

            @pl.when(c == k)
            def _():
                line = prior[...]
                for i in (1, 2, 3):
                    frm = (r + i) % 4
                    dg_copy(i, frm).wait_recv()
                    line = line + dgr[frm, 0:1, :]
                a = lax.broadcasted_iota(jnp.int32, (512, 512), 0)
                b = lax.broadcasted_iota(jnp.int32, (512, 512), 1)
                own = jnp.sum(jnp.where(a == b, f_out[0], 0.0), axis=0, keepdims=True)
                own = own + dg[0:1, :]
                f_out[0] = jnp.where(a == b, own + line, f_out[0])

    def rs_sent(k):
        for table in (SEND, MID):
            for row, moves in table[k].items():
                @pl.when(r == row)
                def _():
                    for m in moves:
                        move(k, m[0], m[1], "end").wait_send()
        if k:
            for i in (1, 2, 3):
                pl.when((c == k) & ((r + i) % 4 == k))(dg_copy(i, r).wait_send)

    def f0_copy(half, step):
        return pltpu.make_async_remote_copy(
            f0_out.at[half], f0_out.at[half], f0_send.at[half, step // 2], f0_recv.at[half],
            device_id=pos.along(step), device_id_type=MESH,
        )

    def f0_take(half, rows):
        for row in rows:
            pl.when(r == row)(f0_copy(half, 1).wait_recv)
        if half == 0:
            if 1 in rows: pl.when(r == 1)(f0_copy(0, 3).start)
        elif 3 in rows:
            pl.when(r == 3)(f0_copy(1, 1).start)

    def f0_sent():
        @pl.when(r == 2)
        def _():
            for half in (0, 1):
                for step in (1, 3):
                    f0_copy(half, step).wait_send()
        pl.when(r == 1)(f0_copy(0, 3).wait_send)
        pl.when(r == 3)(f0_copy(1, 1).wait_send)

    C0 = 20

    def both(t):
        band_slot(t)
        pl.when((t >= C0) & (t < C0 + NC + 5 * SKEW))(lambda: corner_slot(t - C0))

    def slots(a, b):
        loop(b, both, a)

    def product(k, t=None):
        bands[TILES.index(k)].take()
        for half in (0, 1):
            def one(n):
                piece(k, half, n)
                if t is not None: both(t + 2 * half + n)
            loop(2, one)

    slots(0, 2)
    corner_part()
    slots(2, 12)
    own_tile()
    corner_sum()
    slots(12, C0)
    corner_take()
    P0 = NCH + 5 * SKEW
    slots(C0, P0 + 1)
    product(0, P0 + 1)
    rs_send(0)
    slots(P0 + 5, P0 + NCH + 1)
    product(2, P0 + NCH + 1)
    rs_send(2)
    slots(P0 + NCH + 5, P0 + 2 * NCH + 1)
    product(1, P0 + 2 * NCH + 1)
    rs_send(1)
    rs_mid(0)
    slots(P0 + 2 * NCH + 5, T)
    rs_mid(2)
    rs_end(0)
    product(3)
    corners.take()
    rs_send(3)
    rs_mid(1)
    for q in range(4):
        linv[128 * q:128 * (q + 1), :] = corner[q]
    beside = lambda j: lambda p: pl.when(r != 0)(lambda: f0r_slot(p + 8 * j))
    invert_step(linv, 0)
    rs_mid(3)
    invert_step(linv, 1)
    f0_take(0, (1, 3))
    invert_step(linv, 2, beside(0))
    f0_take(1, (1, 3))
    invert_step(linv, 3, beside(1))

    @pl.when(r != 0)
    def _():
        loop(NR + 5 * SKEWR, f0r_slot, 16)
        f0r_own()
        f0rs.take()

    f0_take(0, (0,))
    f0_take(1, (0,))
    for k in (1, 2, 3):
        rs_end(k)

    for spread in bands: spread.sent()
    corners.sent()
    pl.when(r != 0)(f0rs.sent)
    for k in range(4):
        rs_sent(k)
    f0_sent()
    corner_sent()


def gather(jt, w0, w1, wrow, prior):
    dma = pltpu.SemaphoreType.DMA
    return pl.pallas_call(
        gather_kernel,
        out_shape=[
            jax.ShapeDtypeStruct((2, 512, 512), F32),
            jax.ShapeDtypeStruct((2, 512, 512), BF16),
            jax.ShapeDtypeStruct((512, 512), BF16),
            jax.ShapeDtypeStruct((4, 128, 512), F32),
            jax.ShapeDtypeStruct((512, 512), F32),
        ],
        in_specs=[VMEM] * 5,
        out_specs=[VMEM] * 5,
        scratch_shapes=[
            pltpu.VMEM((4, 4, 512, 512), BF16),
            pltpu.VMEM((4, 2, 512, 512), BF16),
            pltpu.VMEM((4, 2, 512, 512), BF16),
            pltpu.VMEM((2, 2, 2, 512, 512), BF16),
            pltpu.VMEM((2, 512, 512), F32),
            pltpu.VMEM((4, 128, 512), F32),
            pltpu.VMEM((4, 128, 512), F32),
            pltpu.VMEM((8, 512), F32),
            pltpu.VMEM((4, 8, 512), F32),
            dma((4, 3, 4, NCH)), dma((4, 4, NCH)), dma((4, 4)), dma((4, 4)),
            dma((3, 4, NC)), dma((4, NC)), dma((4,)), dma((4,)),
            dma((3, 4, NR)), dma((4, NR)), dma((4,)), dma((4,)),
            dma((4, 2)), dma((4, 2)), dma((2, 2, 2)), dma((2, 2)), dma((2,)),
            dma((2, 3)), dma((2, 4)), dma, dma((4,)),
        ],
        compiler_params=pltpu.CompilerParams(
            collective_id=0, has_side_effects=True, vmem_limit_bytes=58 * 2**20
        ),
        cost_estimate=pl.CostEstimate(flops=2 * 2048 * 2048 * 1024, bytes_accessed=2**24, transcendentals=0),
    )(jt, w0, w1, wrow, prior)


def split3(x):
    a = x.astype(BF16)
    rest = x - a.astype(F32)
    b = rest.astype(BF16)
    return a, b, (rest - b.astype(F32)).astype(BF16)


def invert_tile(m, size=16, beside=None):
    lane = lax.broadcasted_iota(jnp.int32, (size, 128), 1)
    row = lax.broadcasted_iota(jnp.int32, (size, 128), 0)
    rows = lax.broadcasted_iota(jnp.int32, (128, 128), 0)
    lanes = lax.broadcasted_iota(jnp.int32, (128, 128), 1)
    spread = lambda v: jnp.broadcast_to(v, (size, 128))

    def panel(p, m):
        if beside is not None:
            beside(p)
        active = 128 - size * p
        x = m[:size]
        cols = [spread(x[:, j:j + 1]) for j in range(size)]
        pivots = jnp.zeros((size, 128), F32)
        d = spread(cols[0][0:1])
        for j in range(size):
            q = pl.reciprocal(d, approx=True)
            q = q * (2.0 - d * q)
            pivots = jnp.where(row == j, d, pivots)
            below = jnp.where(row > j, cols[j], 0.0)
            if j + 1 < size:
                d = spread(cols[j + 1][j + 1:j + 2]) - q * (
                    spread(cols[j][j + 1:j + 2]) * spread(cols[j + 1][j:j + 1])
                )
            u = spread(jnp.where(lane[:1] == j, 1.0, x[j:j + 1]))
            x = jnp.where((lane == j) & (row >= j), jnp.where(row == j, 1.0, 0.0), x)
            x = x - q * (below * u)
            for k in range(j + 1, size):
                cols[k] = cols[k] - q * (below * spread(cols[k][j:j + 1]))
        s = lax.rsqrt(pivots)
        x = x * (s * (1.5 - 0.5 * pivots * s * s))
        x = jnp.where((lane < size) & (lane > row), 0.0, x)
        left = jnp.where((lane >= size) & (lane < active), x, 0.0)
        x1, x2, x3 = split3(x)
        y1, y2, y3 = split3(left)
        update = dotp(
            jnp.concatenate([y1, y1, y2, y2, y1, y3], axis=0),
            jnp.concatenate([x1, x2, x1, x2, x3, x1], axis=0), 0, 0,
        )
        m = jnp.where((lanes < size) & (rows < active), 0.0, m) - update
        m = jnp.concatenate([m[size:], x], axis=0)
        return pltpu.roll(m, 128 - size, 1)

    m = lax.fori_loop(0, 128 // size, panel, m)
    return jnp.where(rows >= lanes, m, 0.0)


def invert_step(a, j, beside=None):
    here = slice(128 * j, 128 * (j + 1))
    t = invert_tile(a[here, here], beside=beside)
    a[here, here] = t
    if j > 0:
        a[here, 0:128 * j] = dotp(t, a[here, 0:128 * j], precision=HIGHEST)
    if j < 3:
        low = 128 * (j + 1)
        a[here, low:] = dotp(t, a[here, low:], precision=HIGHEST)
        u = a[here, :]
        lanes = lax.broadcasted_iota(jnp.int32, (512 - low, 512), 1)
        kept = jnp.where((lanes >= 128 * j) & (lanes < low), 0.0, a[low:, :])
        a[low:, :] = kept - dotp(u[:, low:], u, 0, 0, precision=HIGHEST)
    else:
        rows = lax.broadcasted_iota(jnp.int32, (512, 512), 0)
        lanes = lax.broadcasted_iota(jnp.int32, (512, 512), 1)
        a[...] = jnp.where(rows >= lanes, a[...], 0.0)


def dot3(a, b, ca=1, cb=0):
    return dotp(a[0], b[0], ca, cb) + (dotp(a[0], b[1], ca, cb) + dotp(a[1], b[0], ca, cb))


def pair(x):
    a = x.astype(BF16)
    return a, (x - a.astype(F32)).astype(BF16)


def finish_kernel(f, f0, f0r, corner, inverse, out, res, sem):
    r, c = lax.axis_index("row"), lax.axis_index("col")
    linv = pair(inverse[...])

    def put(half):
        return pltpu.make_async_copy(res.at[half], out.at[:, half, :], sem.at[half])

    def panel(half):
        return dotp(linv[0], f0[half]) + dotp(linv[1], f0[half])

    @pl.when(r == 0)
    def _():
        @pl.when(c == 0)
        def _():
            res[0] = dot3(linv, pair(corner[...].reshape(512, 512)))

        @pl.when(c != 0)
        def _():
            res[0] = panel(0)
        put(0).start()
        res[1] = panel(1)
        put(1).start()

    @pl.when(r != 0)
    def _():
        right = pair(dotp(linv[0], f0r[...]) + dotp(linv[1], f0r[...]))

        @pl.when(c == 0)
        def _():
            res[0] = f[0]

        @pl.when(c != 0)
        def _():
            res[0] = f[0] - dot3(right, pair(panel(0)), 0, 0)
        put(0).start()
        res[1] = f[1] - dot3(right, pair(panel(1)), 0, 0)
        put(1).start()

    for half in (0, 1):
        put(half).wait()


def finish(f, f0, f0r, corner, inverse):
    return pl.pallas_call(
        finish_kernel,
        out_shape=jax.ShapeDtypeStruct((512, 2, 512), F32),
        in_specs=[VMEM] * 5,
        out_specs=pl.BlockSpec(memory_space=pl.ANY),
        scratch_shapes=[
            pltpu.VMEM((2, 512, 512), F32),
            pltpu.SemaphoreType.DMA((2,)),
        ],
        compiler_params=pltpu.CompilerParams(vmem_limit_bytes=56 * 2**20),
        cost_estimate=pl.CostEstimate(flops=2**31, bytes_accessed=2**23, transcendentals=0),
    )(f, f0, f0r, corner, inverse)


def body(sensitivity, sample_weight, pattern, prior):
    blocks = pattern.shape[0]
    x = sensitivity.reshape(blocks * 512, 1024)
    mask = jnp.repeat(pattern[:, :, 0].astype(F32), 512, axis=0)
    scale = sample_weight[:, None] * mask
    w = [
        (scale[:, i:i + 1] * x[:, 512 * i:512 * (i + 1)].astype(F32)).astype(BF16).reshape(blocks, 512, 512)
        for i in (0, 1)
    ]
    jt = (x[:, :512] * mask[:, 0:1].astype(BF16)).reshape(blocks, 512, 512).transpose(0, 2, 1)
    f, f0, f0r, corner, inverse = gather(
        jt, w[0], w[1], sample_weight.reshape(blocks, 1, 512), prior.reshape(1, 512)
    )
    return finish(f, f0, f0r, corner, inverse)


def solution(mesh):
    return jax.shard_map(
        body,
        mesh=mesh,
        in_specs=(P("row", None, "col"), P("row"), P("row", None, "col"), P("row")),
        out_specs=P("row", None, "col"),
        check_vma=False,
    )
```
